256 devices in a mesh: dp: 2 (over core), ctx: 128 (over y, x, z).
Axes of the slice: x: 4, y: 4, z: 8, core: 2. Of those that a mesh axis runs over, the one named last changes fastest.
Arguments:
- features: bfloat16 [2, 32768, 2560], P('dp', 'ctx'), may hold values from -6 to 6
- write_keys: bfloat16 [2, 32768, 128], P('dp', 'ctx'), may hold values from -0.75 to 0.75
- read_queries: bfloat16 [2, 32768, 128], P('dp', 'ctx'), may hold values from -0.75 to 0.75
- step_logits: float32 [2, 40, 32768], P('dp', None, 'ctx'), may hold values from -6 to 6
- step_bias: float32 [40], replicated, may hold values from -1 to 1
- decay_log: float32 [40], replicated, may hold values from -16 to -2
- skip_gain: float32 [40], replicated, may hold values from 0.5 to 1.5
- doc_starts: int32 [2, 32], P('dp'), may hold values from 0 to 32767, as said below
- out_grad: bfloat16 [2, 32768, 2560], P('dp', 'ctx'), may hold values from -20 to 20
Outputs:
- mixed: bfloat16 [2, 32768, 2560], P('dp', 'ctx')
- feature_grad: bfloat16 [2, 32768, 2560], P('dp', 'ctx')
- write_grad: bfloat16 [2, 32768, 128], P('dp', 'ctx')
- read_grad: bfloat16 [2, 32768, 128], P('dp', 'ctx')
- step_grad: float32 [2, 40, 32768], P('dp', None, 'ctx')
- bias_grad: float32 [40], replicated
- decay_grad: float32 [40], replicated
- skip_grad: float32 [40], replicated
The draws below stay inside these ranges and needn't reach their ends.
Inputs may be any that keep to these rules, and one draw needn't show every extreme that they name: `doc_starts`: each row is ascending with distinct entries, begins with 0 and ends with 32767; row b holds the first positions of the documents packed into sequence b.
All inputs are finite; a program needn't handle non-finite values.
Results may differ from the reference program's by a relative error of at most 0.002.
Values sent between devices are 32-bit elements; how exact they have to be, the bound alone decides.
A program may use at most 128 MiB of HBM per device.

```python
import math
import jax
import jax.numpy as jnp
from jax import lax

HEADS = 40
HEAD_DIM = 64
STATE = 128
GROUP_HEADS = 2
L_DEV = 256
BATCH = 2
SEQ = 32768
DOCS = 32
N_CTX = 128


def draw_decay_log(key, part):
    key = jax.random.fold_in(key, 11)
    uniform_draw = jax.random.uniform(key, (HEADS,), jnp.float32)
    lowest = math.log(1.0 / SEQ)
    highest = math.log(0.05)
    return (lowest + uniform_draw * (highest - lowest)).astype(jnp.float32)


def draw_doc_starts(key, part):
    key = jax.random.fold_in(key, 23)
    window = SEQ // 4

    def one_row(row_key):
        side_bit = jax.random.randint(jax.random.fold_in(row_key, 1), (), 0, 2)
        window_start = jnp.where(side_bit == 1, SEQ - 1 - window, 1).astype(jnp.int32)
        chosen = jax.random.permutation(jax.random.fold_in(row_key, 2), window)[:DOCS - 2].astype(jnp.int32) + window_start
        inner = jnp.sort(chosen)
        return jnp.concatenate([jnp.zeros((1,), jnp.int32), inner, jnp.full((1,), SEQ - 1, jnp.int32)])
    return jax.vmap(one_row)(jax.random.split(key, BATCH))


def draw_out_grad(key, part):
    key = jax.random.fold_in(key, 37)
    shape_all = (BATCH, SEQ, HEADS * HEAD_DIM)
    ramp = 1.0 + 2.0 * jnp.arange(SEQ, dtype=jnp.float32) / SEQ
    values = jnp.clip(jax.random.normal(key, shape_all, jnp.float32), -6.0, 6.0) * ramp[None, :, None]
    return values.astype(jnp.bfloat16)


def block_levels(own_key, shape, cuts, low, top_value):
    level = 1.0
    for axis_at, parts in cuts:
        heights = jax.random.uniform(jax.random.fold_in(jax.random.fold_in(own_key, 6), axis_at), (parts,), jnp.float32, low / len(cuts), top_value / len(cuts))
        level = level * jnp.repeat(jnp.exp(heights), shape[axis_at] // parts).reshape((-1,) + (1,) * (len(shape) - 1 - axis_at))
    return level


def normal_values(rng, extent, spread, most, shards=(), kind=jnp.bfloat16):
    gain = block_levels(rng, extent, shards, -0.22, 0.18) if shards else 1.0
    values = jax.random.normal(rng, extent, jnp.float32) * spread * gain
    return jnp.minimum(jnp.maximum(values, -most), most).astype(kind)


def setup_inputs(seed: int = 0) -> dict:
    streams_of = jax.random.split(jax.random.key(seed), 10)
    return {
        "features": normal_values(streams_of[0], (BATCH, SEQ, HEADS * HEAD_DIM), 1.0, 6.0, ((0, 2), (1, 128))),
        "write_keys": normal_values(streams_of[1], (BATCH, SEQ, STATE), (1.0 / (4 * STATE * L_DEV) ** 0.25), 0.75, ((0, 2), (1, 128))),
        "read_queries": normal_values(streams_of[2], (BATCH, SEQ, STATE), (1.0 / (4 * STATE * L_DEV) ** 0.25), 0.75, ((0, 2), (1, 128))),
        "step_logits": normal_values(streams_of[3], (BATCH, HEADS, SEQ), 1.0, 6.0, ((0, 2), (2, 128)), jnp.float32),
        "step_bias": jnp.clip(jax.random.uniform(streams_of[4], (HEADS,), jnp.float32, -1.0, 1.0), -1.0, 1.0),
        "decay_log": draw_decay_log(jax.random.fold_in(streams_of[9], 71), 0),
        "skip_gain": jnp.clip(jax.random.uniform(streams_of[6], (HEADS,), jnp.float32, 0.5, 1.5), 0.5, 1.5),
        "doc_starts": draw_doc_starts(jax.random.fold_in(streams_of[9], 71), 0),
        "out_grad": draw_out_grad(jax.random.fold_in(streams_of[9], 71), 0),
    }


EXACT = lax.Precision.HIGHEST

def widen(values, repeat_by):
    return jnp.repeat(values, repeat_by, axis=-1)

def step_decays(logit_block, step_bias, decay_log):
    stride = jax.nn.softplus(logit_block + step_bias[:, None])
    decay_rate = -jnp.exp(decay_log)
    cumulative = jnp.cumsum(stride * decay_rate[:, None], axis=1)
    return (stride, cumulative)

def segments(doc_starts, start_pos, length):
    positions = start_pos + jnp.arange(length, dtype=jnp.int32)
    segment = lax.optimization_barrier(jnp.sum((doc_starts[None, :] <= positions[:, None]).astype(jnp.int32), axis=1))
    entry_segment = jnp.sum((doc_starts <= start_pos - 1).astype(jnp.int32))
    return (segment, entry_segment)

def block_state(feature_block, write_block, logit_block, step_bias, decay_log, own_last, linked):
    stride, cumulative = step_decays(logit_block, step_bias, decay_log)
    weights = own_last[None, :] * jnp.exp(cumulative[:, -1:] - cumulative) * stride
    head_size = feature_block.shape[1] // stride.shape[0]
    scaled = feature_block * widen(weights.T, head_size)
    state_end = jnp.dot(write_block.T, scaled, precision=EXACT, preferred_element_type=jnp.float32)
    totals = jnp.exp(cumulative[:, -1]) * linked
    return (state_end, totals)

def intra_group(cum_group, stride_group, feature_group, scores, same_doc):
    gaps = cum_group[:, :, None] - cum_group[:, None, :]
    decays = jnp.exp(jnp.where(same_doc[None], gaps, -jnp.inf))
    mixing = decays * scores[None] * stride_group[:, None, :]
    head_count = cum_group.shape[0]
    per_head = feature_group.reshape(feature_group.shape[0], head_count, -1)
    result = jnp.einsum('htu,uhp->thp', mixing, per_head, precision=EXACT)
    return result.reshape(feature_group.shape[0], -1)

def block_main(feature_block, write_block, read_block, logit_block, step_bias, decay_log, skip_gain, segment):
    stride, cumulative = step_decays(logit_block, step_bias, decay_log)
    length = feature_block.shape[0]
    head_count = stride.shape[0]
    head_size = feature_block.shape[1] // head_count
    groups = head_count // GROUP_HEADS
    ordinal = jnp.arange(length, dtype=jnp.int32)
    same_doc = (segment[:, None] == segment[None, :]) & (ordinal[:, None] >= ordinal[None, :])
    scores = jnp.dot(read_block, write_block.T, precision=EXACT, preferred_element_type=jnp.float32)
    cum_stack = cumulative.reshape(groups, GROUP_HEADS, length)
    stride_stack = stride.reshape(groups, GROUP_HEADS, length)
    feature_stack = feature_block.reshape(length, groups, GROUP_HEADS * head_size).transpose(1, 0, 2)

    def one_group(packed):
        return intra_group(packed[0], packed[1], packed[2], scores, same_doc)
    pieces = lax.map(jax.checkpoint(one_group), (cum_stack, stride_stack, feature_stack))
    inside = pieces.transpose(1, 0, 2).reshape(length, -1)
    return inside + feature_block * widen(skip_gain, head_size)

def block_carry(read_block, logit_block, step_bias, decay_log, keep_in, state_in):
    stride, cumulative = step_decays(logit_block, step_bias, decay_log)
    factor = keep_in[:, None] * jnp.exp(cumulative.T)
    head_size = state_in.shape[1] // factor.shape[1]
    return jnp.dot(read_block, state_in, precision=EXACT, preferred_element_type=jnp.float32) * widen(factor, head_size)

def sequence_forward(features, write_keys, read_queries, step_logits, step_bias, decay_log, skip_gain, doc_starts):
    head_count = step_logits.shape[0]
    feature_blocks = features.reshape(N_CTX, L_DEV, -1)
    write_blocks = write_keys.reshape(N_CTX, L_DEV, -1)
    read_blocks = read_queries.reshape(N_CTX, L_DEV, -1)
    logit_blocks = step_logits.reshape(head_count, N_CTX, L_DEV).transpose(1, 0, 2)
    offsets = jnp.arange(N_CTX, dtype=jnp.int32) * L_DEV
    head_size = features.shape[1] // head_count

    def advance(carried, packed):
        feature_block, write_block, read_block, logit_block, start_pos = packed
        segment, entry_segment = segments(doc_starts, start_pos, L_DEV)
        keep_in = (segment == entry_segment).astype(jnp.float32)
        own_last = (segment == segment[-1]).astype(jnp.float32)
        linked = (segment[-1] == entry_segment).astype(jnp.float32)
        result = block_main(feature_block, write_block, read_block, logit_block, step_bias, decay_log, skip_gain, segment)
        result = result + block_carry(read_block, logit_block, step_bias, decay_log, keep_in, carried)
        state_end, totals = block_state(feature_block, write_block, logit_block, step_bias, decay_log, own_last, linked)
        carried = carried * widen(totals, head_size)[None, :] + state_end
        return (carried, result)
    initial = jnp.zeros((write_keys.shape[1], features.shape[1]), jnp.float32)
    _, outputs = lax.scan(jax.checkpoint(advance), initial, (feature_blocks, write_blocks, read_blocks, logit_blocks, offsets))
    return outputs.reshape(features.shape[0], -1)

def reference(features, write_keys, read_queries, step_logits, step_bias, decay_log, skip_gain, doc_starts, out_grad):
    mixed_rows, feature_rows, write_rows, read_rows, step_rows = ([], [], [], [], [])
    bias_total = jnp.zeros_like(step_bias)
    decay_total = jnp.zeros_like(decay_log)
    skip_total = jnp.zeros_like(skip_gain)
    for member in range(features.shape[0]):
        starts_row = doc_starts[member]

        def sequence_fn(feat_in, write_in, read_in, logit_in, bias_in, decay_in, skip_in, starts_row=starts_row):
            return sequence_forward(feat_in, write_in, read_in, logit_in, bias_in, decay_in, skip_in, starts_row)
        mixed_out, pullback = jax.vjp(sequence_fn, features[member].astype(jnp.float32), write_keys[member].astype(jnp.float32), read_queries[member].astype(jnp.float32), step_logits[member], step_bias, decay_log, skip_gain)
        gradients = pullback(out_grad[member].astype(jnp.float32))
        mixed_rows.append(mixed_out.astype(jnp.bfloat16))
        feature_rows.append(gradients[0].astype(jnp.bfloat16))
        write_rows.append(gradients[1].astype(jnp.bfloat16))
        read_rows.append(gradients[2].astype(jnp.bfloat16))
        step_rows.append(gradients[3])
        bias_total = bias_total + gradients[4]
        decay_total = decay_total + gradients[5]
        skip_total = skip_total + gradients[6]
    return (jnp.stack(mixed_rows), jnp.stack(feature_rows), jnp.stack(write_rows), jnp.stack(read_rows), jnp.stack(step_rows), bias_total, decay_total, skip_total)
```

```python
import functools

import jax
import jax.numpy as jnp
from jax import lax
from jax.experimental import pallas as pl
from jax.experimental.pallas import tpu as pltpu
from jax.sharding import PartitionSpec as P

MESH = pl.DeviceIdType.MESH
F32 = jnp.float32
BF16 = jnp.bfloat16
EXACT = lax.Precision.HIGHEST

HEADS = 40
PAIRS = 20
PAD = 24
HALF = 64
LEN = 256
WIDE = 2560
CHUNKS = 40
NY, NX, NZ = 4, 4, 8
HOP = 2
NEG = -1e30


def split2(value):
    high = value.astype(BF16)
    return high, (value - high.astype(F32)).astype(BF16)


def split3(value):
    high = value.astype(BF16)
    rest = value - high.astype(F32)
    middle = rest.astype(BF16)
    return high, middle, (rest - middle.astype(F32)).astype(BF16)


def mm(left, right):
    return jnp.dot(left, right, preferred_element_type=F32)


def mm_nt(left, right):
    return lax.dot_general(left, right, (((1,), (1,)), ((), ())), preferred_element_type=F32)


def mm_tn(left, right):
    return lax.dot_general(left, right, (((0,), (0,)), ((), ())), preferred_element_type=F32)


def iota(shape, axis):
    return lax.broadcasted_iota(jnp.int32, shape, axis)


def to_column(row):
    size = row.shape[1]
    eye = iota((size, size), 0) == iota((size, size), 1)
    return jnp.sum(jnp.where(eye, row, 0.0), axis=1, keepdims=True)


def to_row(column):
    size = column.shape[0]
    eye = iota((size, size), 0) == iota((size, size), 1)
    return jnp.sum(jnp.where(eye, column, 0.0), axis=0, keepdims=True)


def pair_rows(column):
    wide = jnp.broadcast_to(column, (HEADS, 128))
    head = iota((PAD, HEADS), 1)
    row = iota((PAD, HEADS), 0)
    even = jnp.dot((head == 2 * row).astype(F32), wide, precision=EXACT, preferred_element_type=F32)
    odd = jnp.dot((head == 2 * row + 1).astype(F32), wide, precision=EXACT, preferred_element_type=F32)
    return jnp.where(iota((PAD, 128), 1) < HALF, even, odd)


def unpair_sums(rows):
    first = jnp.sum(jnp.where(iota((PAD, 128), 1) < HALF, rows, 0.0), axis=1, keepdims=True)
    second = jnp.sum(jnp.where(iota((PAD, 128), 1) < HALF, 0.0, rows), axis=1, keepdims=True)
    head = iota((HEADS, PAD), 0)
    row = iota((HEADS, PAD), 1)
    first = jnp.broadcast_to(first, (PAD, 128))
    second = jnp.broadcast_to(second, (PAD, 128))
    total = jnp.dot((head == 2 * row).astype(F32), first, precision=EXACT, preferred_element_type=F32)
    total += jnp.dot((head == 2 * row + 1).astype(F32), second, precision=EXACT, preferred_element_type=F32)
    return total[:, 0:1]


def spread_columns(rows):
    high, middle, low = split3(rows)
    head = iota((HEADS, WIDE), 0)
    lane = iota((HEADS, WIDE), 1)
    expand = (lane // HALF == head).astype(BF16)
    return mm_tn(high, expand) + (mm_tn(middle, expand) + mm_tn(low, expand))


def steps(logits, bias_row, decay_row):
    bias = to_column(bias_row)
    rate = -jnp.exp(to_column(decay_row))
    shifted = logits + bias
    stride = jnp.maximum(shifted, 0.0) + jnp.log1p(jnp.exp(-jnp.abs(shifted)))
    return shifted, stride, rate


def before_kernel(
    docs_ref,
    x_ref,
    dy_ref,
    b_ref,
    c_ref,
    logit_ref,
    bias_ref,
    decay_ref,
    state_ref,
    lam_ref,
    y_ref,
    dx_ref,
    dg_ref,
    wide_w,
    wide_f,
    wide_l,
    wide_m,
    row_l,
    row_m,
    gram,
    gram_t,
    mask,
    mask_t,
    b_t,
    c_t,
):
    position = lax.axis_index("ctx")
    start = position * LEN
    shifted, stride, rate = steps(logit_ref[...], bias_ref[...], decay_ref[...])
    upper = (iota((LEN, LEN), 0) <= iota((LEN, LEN), 1)).astype(F32)
    total = jnp.dot(stride * rate, upper, precision=EXACT, preferred_element_type=F32)
    last = total[:, LEN - 1 : LEN]

    seg_row = jnp.zeros((1, LEN), jnp.int32)
    seg_col = jnp.zeros((LEN, 128), jnp.int32)
    entry = jnp.int32(0)
    final = jnp.int32(0)
    for d in range(docs_ref.shape[1]):
        doc = docs_ref[0, d] - start
        seg_row += (doc <= iota((1, LEN), 1)).astype(jnp.int32)
        seg_col += (doc <= iota((LEN, 128), 0)).astype(jnp.int32)
        entry += (doc <= -1).astype(jnp.int32)
        final += (doc <= LEN - 1).astype(jnp.int32)
    seg_col = seg_col[:, 0:1]
    same = seg_col == seg_row
    mask[...] = jnp.where(same & (iota((LEN, LEN), 0) >= iota((LEN, LEN), 1)), 0.0, NEG)
    mask_t[...] = jnp.where(same & (iota((LEN, LEN), 0) <= iota((LEN, LEN), 1)), 0.0, NEG)
    keep = (seg_row == entry).astype(F32)
    own = (seg_row == final).astype(F32)
    linked = (final == entry).astype(F32)

    weight = own * jnp.exp(last - total) * stride
    factor = keep * jnp.exp(total)
    moved = total - jnp.log(stride)
    row_l[...] = total
    row_m[...] = moved
    wide_w[...] = spread_columns(weight)
    wide_f[...] = spread_columns(factor)
    wide_l[...] = spread_columns(total)
    wide_m[...] = spread_columns(moved)
    lam_ref[...] = pair_rows(jnp.exp(last) * linked)

    b = b_ref[...]
    c = c_ref[...]
    gram[...] = mm_nt(c, b)
    gram_t[...] = mm_nt(b, c)
    b_t[...] = b.astype(F32).T.astype(BF16)
    c_t[...] = c.astype(F32).T.astype(BF16)
    dg_ref[...] = jnp.zeros((LEN, LEN), F32)

    def pair(j, carry):
        lanes = pl.ds(pl.multiple_of(j * 128, 128), 128)
        x = x_ref[:, lanes]
        dy = dy_ref[:, lanes]
        first = iota((LEN, 128), 1) < HALF
        high, low = split2(wide_w[:, lanes] * x.astype(F32))
        state = mm(b_t[...], high) + mm(b_t[...], low)
        high, low = split2(wide_f[:, lanes] * dy.astype(F32))
        state_b = mm(c_t[...], high) + mm(c_t[...], low)
        state_ref[2 * j, 0] = state[:HALF]
        state_ref[2 * j + 1, 0] = state[HALF:]
        state_ref[2 * j, 1] = state_b[:HALF]
        state_ref[2 * j + 1, 1] = state_b[HALF:]
        columns_l = wide_l[:, lanes]
        columns_m = wide_m[:, lanes]
        ys, dxs = [], []
        for k in range(2):
            lrow = row_l[pl.ds(2 * j + k, 1), :]
            mrow = row_m[pl.ds(2 * j + k, 1), :]
            lcol = columns_l[:, k * HALF : k * HALF + 1]
            mcol = columns_m[:, k * HALF : k * HALF + 1]
            decays = jnp.exp((lcol - mrow) + mask[...])
            high, low = split2(decays * gram[...])
            ys.append(mm(high, x) + mm(low, x))
            part = jnp.where(first if k == 0 else ~first, dy, jnp.zeros_like(dy))
            dg_ref[...] += mm_nt(part, x) * decays
            decays_t = jnp.exp((lrow - mcol) + mask_t[...])
            high, low = split2(decays_t * gram_t[...])
            dxs.append(mm(high, dy) + mm(low, dy))
        y_ref[:, lanes] = jnp.where(first, ys[0], ys[1])
        dx_ref[:, lanes] = jnp.where(first, dxs[0], dxs[1])
        return carry

    lax.fori_loop(0, PAIRS, pair, 0)


def place():
    index = lax.axis_index("ctx")
    return index // (NX * NZ), (index // NZ) % NX, index % NZ


def at(y, x, z):
    return (lax.axis_index("dp"), (y * NX + x) * NZ + z)


def partner(i):
    return i + 1 - 2 * (i % 2)


def scan_kernel(
    state_ref,
    lam_ref,
    out_ref,
    up_in,
    up_out,
    down_in,
    down_out,
    t_out,
    x1_in,
    u2_out,
    x2_in,
    u_out,
    y1_in,
    v2_out,
    y2_in,
    zlam,
    xlam,
    ylam,
    coef,
    send_sem,
    recv_sem,
    small_send,
    small_recv,
):
    y, x, z = place()
    barrier = pltpu.get_barrier_semaphore()
    peers = [at(y, x, (z + k) % NZ) for k in range(1, NZ)]
    peers += [at(y, (x + k) % NX, z) for k in range(1, NX)]
    peers += [at((y + k) % NY, x, z) for k in range(1, NY)]
    for peer in peers:
        pl.semaphore_signal(barrier, inc=1, device_id=peer, device_id_type=MESH)
    pl.semaphore_wait(barrier, len(peers))

    def gather(table, own, size, value, targets, offset):
        table[own] = value
        copies = []
        for k, target in enumerate(targets):
            copy = pltpu.make_async_remote_copy(
                src_ref=table.at[own],
                dst_ref=table.at[own],
                send_sem=small_send.at[offset + k],
                recv_sem=small_recv.at[offset + k],
                device_id=target,
                device_id_type=MESH,
            )
            copy.start()
            copies.append(copy)
        for k, copy in enumerate(copies):
            source = (own + size - 1 - k) % size
            pltpu.make_async_remote_copy(
                src_ref=table.at[source],
                dst_ref=table.at[source],
                send_sem=small_send.at[offset + k],
                recv_sem=small_recv.at[offset + k],
                device_id=targets[k],
                device_id_type=MESH,
            ).wait_recv()
        for copy in copies:
            copy.wait_send()

    one = jnp.ones((PAD, 128), F32)
    zero = jnp.zeros((PAD, 128), F32)

    def products(table, own, size):
        below, above = one, one
        for k in range(size):
            below *= jnp.where(own > k, table[k], one)
            above *= jnp.where(own < k, table[k], one)
        return below, above

    gather(zlam, z, NZ, lam_ref[...], peers[:7], 0)
    below_z, above_z = products(zlam, z, NZ)
    group = below_z * above_z * lam_ref[...]
    gather(xlam, x, NX, group, peers[7:10], 7)
    below_x, above_x = products(xlam, x, NX)
    plane = below_x * above_x * group
    gather(ylam, y, NY, plane, peers[10:13], 10)

    def ring_of_four(table, own):
        mine, other = table[own], table[partner(own)]
        both = mine * other
        across = table[3 - own] * table[partner(3 - own)]
        odd = own % 2 == 1
        upper = own >= 2
        forward = (
            jnp.where(odd, one, other),
            jnp.where(odd, mine, one),
            jnp.where(odd, one, zero),
            jnp.where(upper, one, across),
            jnp.where(upper, both, one),
            jnp.where(upper, jnp.where(odd, other, one), zero),
        )
        backward = (
            jnp.where(odd, other, one),
            jnp.where(odd, one, mine),
            jnp.where(odd, zero, one),
            jnp.where(upper, across, one),
            jnp.where(upper, one, both),
            jnp.where(upper, zero, jnp.where(odd, one, other)),
        )
        return forward, backward

    in_x = ring_of_four(xlam, x)
    in_y = ring_of_four(ylam, y)
    for d in range(2):
        outer, inner = (below_z, above_z) if d == 0 else (above_z, below_z)
        outer_x = outer * (below_x if d == 0 else above_x)
        table = (
            lam_ref[...],
            inner,
            in_x[d][0],
            in_x[d][1],
            in_x[d][3],
            in_x[d][4],
            in_y[d][0],
            in_y[d][1],
            outer * in_x[d][2],
            outer * in_x[d][5],
            outer_x * in_y[d][2],
            outer_x * in_y[d][5],
        )
        for k, value in enumerate(table):
            coef[d, k] = value

    @pl.when(z == 0)
    def _():
        up_in[...] = jnp.zeros_like(up_in)

    @pl.when(z == NZ - 1)
    def _():
        down_in[...] = jnp.zeros_like(down_in)

    to_up = at(y, x, (z + 1) % NZ)
    to_down = at(y, x, (z + NZ - 1) % NZ)
    to_x1 = at(y, partner(x), z)
    to_x2 = at(y, 3 - x, z)
    to_y1 = at(partner(y), x, z)
    to_y2 = at(3 - y, x, z)

    def link(stage, c, source, target, device):
        return pltpu.make_async_remote_copy(
            src_ref=source.at[c],
            dst_ref=target.at[c],
            send_sem=send_sem.at[stage, c],
            recv_sem=recv_sem.at[stage, c],
            device_id=device,
            device_id_type=MESH,
        )

    links = (
        functools.partial(link, 0, source=up_out, target=up_in, device=to_up),
        functools.partial(link, 1, source=down_out, target=down_in, device=to_down),
        functools.partial(link, 2, source=t_out, target=x1_in, device=to_x1),
        functools.partial(link, 3, source=u2_out, target=x2_in, device=to_x2),
        functools.partial(link, 4, source=u_out, target=y1_in, device=to_y1),
        functools.partial(link, 5, source=v2_out, target=y2_in, device=to_y2),
    )

    def staged(c):
        return (c >= 0) & (c < CHUNKS)

    lag_t = HOP * jnp.maximum(z, NZ - 1 - z)

    def tick(i, carry):
        def row(d, k, c):
            return coef[d, k, pl.ds(c // 2, 1), :]

        c_up = i - HOP * z

        @pl.when(staged(c_up))
        def _():
            @pl.when(z > 0)
            def _():
                links[0](c_up).wait_recv()

            up_out[c_up, 0] = row(0, 0, c_up) * up_in[c_up, 0] + state_ref[c_up, 0]
            up_out[c_up, 1] = up_in[c_up, 1] + row(1, 1, c_up) * state_ref[c_up, 1]

            @pl.when(z < NZ - 1)
            def _():
                links[0](c_up).start()

        c_down = i - HOP * (NZ - 1 - z)

        @pl.when(staged(c_down))
        def _():
            @pl.when(z < NZ - 1)
            def _():
                links[1](c_down).wait_recv()

            down_out[c_down, 0] = down_in[c_down, 0] + row(0, 1, c_down) * state_ref[c_down, 0]
            down_out[c_down, 1] = row(1, 0, c_down) * down_in[c_down, 1] + state_ref[c_down, 1]

            @pl.when(z > 0)
            def _():
                links[1](c_down).start()

        c_t = i - lag_t

        @pl.when(staged(c_t))
        def _():
            t_out[c_t, 0] = up_out[c_t, 0] * row(0, 1, c_t) + down_in[c_t, 0]
            t_out[c_t, 1] = down_out[c_t, 1] * row(1, 1, c_t) + up_in[c_t, 1]
            links[2](c_t).start()

        for stage, mine, came, result, k in (
            (2, t_out, x1_in, u2_out, 2),
            (3, u2_out, x2_in, u_out, 4),
            (4, u_out, y1_in, v2_out, 6),
        ):
            c = c_t - HOP * (stage - 1)

            @pl.when(staged(c))
            def _(stage=stage, mine=mine, came=came, result=result, k=k, c=c):
                links[stage](c).wait_recv()
                for d in range(2):
                    result[c, d] = row(d, k, c) * mine[c, d] + row(d, k + 1, c) * came[c, d]
                links[stage + 1](c).start()

        c_end = c_t - HOP * 4

        @pl.when(staged(c_end))
        def _():
            links[5](c_end).wait_recv()
            for d, near in ((0, up_in), (1, down_in)):
                out_ref[c_end, d] = near[c_end, d] + (
                    (row(d, 8, c_end) * x1_in[c_end, d] + row(d, 9, c_end) * x2_in[c_end, d])
                    + (row(d, 10, c_end) * y1_in[c_end, d] + row(d, 11, c_end) * y2_in[c_end, d])
                )

        return carry

    lax.fori_loop(0, CHUNKS + HOP * (NZ - 1 + 4), tick, 0)

    def drain(c, carry):
        @pl.when(z < NZ - 1)
        def _():
            links[0](c).wait_send()

        @pl.when(z > 0)
        def _():
            links[1](c).wait_send()

        for stage in range(2, 6):
            links[stage](c).wait_send()
        return carry

    lax.fori_loop(0, CHUNKS, drain, 0)


def after_kernel(
    docs_ref,
    x_ref,
    dy_ref,
    b_ref,
    c_ref,
    logit_ref,
    bias_ref,
    decay_ref,
    skip_ref,
    wide_w,
    wide_f,
    state_ref,
    lam_ref,
    in_ref,
    y_ref,
    dx_ref,
    dg_ref,
    mixed_ref,
    feature_ref,
    write_ref,
    read_ref,
    step_ref,
    sums_ref,
    db,
    dc,
    rows_r,
    rows_v,
    row_last,
    row_skip,
    gains,
):
    shifted, stride, rate = steps(logit_ref[...], bias_ref[...], decay_ref[...])
    gains[...] = pair_rows(to_column(skip_ref[...]))
    db[...] = jnp.zeros_like(db)
    dc[...] = jnp.zeros_like(dc)
    row_last[...] = jnp.zeros_like(row_last)
    row_skip[...] = jnp.zeros_like(row_skip)
    b = b_ref[...]
    c = c_ref[...]

    def pair(j, carry):
        lanes = pl.ds(pl.multiple_of(j * 128, 128), 128)
        x = x_ref[:, lanes]
        dy = dy_ref[:, lanes]
        x32 = x.astype(F32)
        dy32 = dy.astype(F32)
        w = wide_w[:, lanes]
        f = wide_f[:, lanes]
        gain = gains[pl.ds(j, 1), :]
        state_in = jnp.concatenate([in_ref[2 * j, 0], in_ref[2 * j + 1, 0]], axis=0)
        adjoint = jnp.concatenate([in_ref[2 * j, 1], in_ref[2 * j + 1, 1]], axis=0)
        state_end = jnp.concatenate([state_ref[2 * j, 0], state_ref[2 * j + 1, 0]], axis=0)
        s_high, s_low = split2(state_in)
        a_high, a_low = split2(adjoint)
        y = y_ref[:, lanes] + f * (mm(c, s_high) + mm(c, s_low))
        dx = dx_ref[:, lanes] + w * (mm(b, a_high) + mm(b, a_low))
        mixed_ref[:, lanes] = (y + gain * x32).astype(BF16)
        feature_ref[:, lanes] = (dx + gain * dy32).astype(BF16)
        select = (iota((8, 128), 1) // HALF == iota((8, 128), 0)).astype(BF16)
        high, middle, low = split3(dy32 * y)
        r = mm_nt(select, high) + (mm_nt(select, middle) + mm_nt(select, low))
        high, middle, low = split3(x32 * dx)
        v = mm_nt(select, high) + (mm_nt(select, middle) + mm_nt(select, low))
        for k in range(2):
            rows_r[pl.ds(2 * j + k, 1), :] = r[k : k + 1]
            rows_v[pl.ds(2 * j + k, 1), :] = v[k : k + 1]
        high, low = split2(f * dy32)
        dc[...] += mm_nt(high, s_high) + (mm_nt(high, s_low) + mm_nt(low, s_high))
        high, low = split2(w * x32)
        db[...] += mm_nt(high, a_high) + (mm_nt(high, a_low) + mm_nt(low, a_high))
        row_skip[pl.ds(j, 1), :] = jnp.sum(dy32 * x32, axis=0, keepdims=True)
        leaving = lam_ref[pl.ds(j, 1), :] * state_in + state_end
        row_last[pl.ds(j, 1), :] = jnp.sum(adjoint * leaving, axis=0, keepdims=True)
        return carry

    lax.fori_loop(0, PAIRS, pair, 0)
    dg = dg_ref[...]
    high, low = split2(dg)
    read_ref[...] = (dc[...] + (mm(high, b) + mm(low, b))).astype(BF16)
    high, low = split2(dg.T)
    write_ref[...] = (db[...] + (mm(high, c) + mm(low, c))).astype(BF16)

    v = rows_v[...]
    is_last = iota((HEADS, LEN), 1) == LEN - 1
    slope = rows_r[...] - v + jnp.where(is_last, unpair_sums(row_last[...]), 0.0)
    lower = (iota((LEN, LEN), 0) >= iota((LEN, LEN), 1)).astype(F32)
    slope = jnp.dot(slope, lower, precision=EXACT, preferred_element_type=F32)
    step = (v / stride + rate * slope) * (1.0 / (1.0 + jnp.exp(-shifted)))
    step_ref[...] = step
    bias_sum = jnp.sum(step, axis=1, keepdims=True)
    decay_sum = jnp.sum(slope * (rate * stride), axis=1, keepdims=True)
    skip_sum = unpair_sums(row_skip[...])
    sums_ref[...] = jnp.concatenate(
        [to_row(bias_sum), to_row(decay_sum), to_row(skip_sum), jnp.zeros((5, HEADS), F32)], axis=0
    )


VM = pl.BlockSpec(memory_space=pltpu.VMEM)
SM = pl.BlockSpec(memory_space=pltpu.SMEM)


def shape(dims, kind=F32):
    return jax.ShapeDtypeStruct(dims, kind)


def local(
    features,
    write_keys,
    read_queries,
    step_logits,
    step_bias,
    decay_log,
    skip_gain,
    doc_starts,
    out_grad,
):
    x, b, c, logits, dy = features[0], write_keys[0], read_queries[0], step_logits[0], out_grad[0]
    bias, decay, skip = step_bias[None], decay_log[None], skip_gain[None]
    carry_shape = (CHUNKS, 2, HALF, 128)
    state, lam, y, dx, dg, wide_w, wide_f = pl.pallas_call(
        before_kernel,
        out_shape=(
            shape(carry_shape),
            shape((PAD, 128)),
            shape((LEN, WIDE)),
            shape((LEN, WIDE)),
            shape((LEN, LEN)),
            shape((LEN, WIDE)),
            shape((LEN, WIDE)),
        ),
        in_specs=[SM] + [VM] * 7,
        out_specs=(VM,) * 7,
        scratch_shapes=[pltpu.VMEM((LEN, WIDE), F32)] * 2
        + [pltpu.VMEM((HEADS, LEN), F32)] * 2
        + [pltpu.VMEM((LEN, LEN), F32)] * 4
        + [pltpu.VMEM((128, LEN), BF16)] * 2,
        compiler_params=pltpu.CompilerParams(vmem_limit_bytes=56 * 2**20),
        name="before",
    )(doc_starts, x, dy, b, c, logits, bias, decay)
    entering = pl.pallas_call(
        scan_kernel,
        out_shape=shape(carry_shape),
        in_specs=[VM] * 2,
        out_specs=VM,
        scratch_shapes=[pltpu.VMEM(carry_shape, F32)] * 12
        + [pltpu.VMEM((NZ, PAD, 128), F32), pltpu.VMEM((NX, PAD, 128), F32), pltpu.VMEM((NY, PAD, 128), F32)]
        + [pltpu.VMEM((2, 12, PAD, 128), F32)]
        + [pltpu.SemaphoreType.DMA((6, CHUNKS))] * 2
        + [pltpu.SemaphoreType.DMA((13,))] * 2,
        compiler_params=pltpu.CompilerParams(
            collective_id=0, has_side_effects=True, vmem_limit_bytes=56 * 2**20
        ),
        name="scan",
    )(state, lam)
    mixed, feature_grad, write_grad, read_grad, step_grad, sums = pl.pallas_call(
        after_kernel,
        out_shape=(
            shape((LEN, WIDE), BF16),
            shape((LEN, WIDE), BF16),
            shape((LEN, 128), BF16),
            shape((LEN, 128), BF16),
            shape((HEADS, LEN)),
            shape((8, HEADS)),
        ),
        in_specs=[SM] + [VM] * 16,
        out_specs=(VM,) * 6,
        scratch_shapes=[pltpu.VMEM((LEN, 128), F32)] * 2
        + [pltpu.VMEM((HEADS, LEN), F32)] * 2
        + [pltpu.VMEM((PAD, 128), F32)] * 3,
        compiler_params=pltpu.CompilerParams(vmem_limit_bytes=56 * 2**20),
        name="after",
    )(doc_starts, x, dy, b, c, logits, bias, decay, skip, wide_w, wide_f, state, lam, entering, y, dx, dg)
    sums = lax.psum(sums, ("dp", "ctx"))
    return (
        mixed[None],
        feature_grad[None],
        write_grad[None],
        read_grad[None],
        step_grad[None],
        sums[0],
        sums[1],
        sums[2],
    )


def solution(mesh):
    in_specs = (
        P("dp", "ctx", None),
        P("dp", "ctx", None),
        P("dp", "ctx", None),
        P("dp", None, "ctx"),
        P(),
        P(),
        P(),
        P("dp", None),
        P("dp", "ctx", None),
    )
    out_specs = (
        P("dp", "ctx", None),
        P("dp", "ctx", None),
        P("dp", "ctx", None),
        P("dp", "ctx", None),
        P("dp", None, "ctx"),
        P(),
        P(),
        P(),
    )
    return jax.shard_map(local, mesh=mesh, in_specs=in_specs, out_specs=out_specs, check_vma=False)
```

```python
import functools

import jax
import jax.numpy as jnp
from jax import lax
from jax.experimental import pallas as pl
from jax.experimental.pallas import tpu as pltpu
from jax.sharding import PartitionSpec as P

MESH = pl.DeviceIdType.MESH
F32 = jnp.float32
BF16 = jnp.bfloat16
EXACT = lax.Precision.HIGHEST

HEADS = 40
PAIRS = 20
PAD = 24
HALF = 64
LEN = 256
WIDE = 2560
CHUNKS = 40
SPLIT = CHUNKS // PAIRS
ROWS = 128 // SPLIT
NY, NX, NZ = 4, 4, 8
HOP = 3
GATHER_X = 3
GATHER_Y = 7
NEG = -1e30


def split2(value):
    high = value.astype(BF16)
    return high, (value - high.astype(F32)).astype(BF16)


def split3(value):
    high = value.astype(BF16)
    rest = value - high.astype(F32)
    middle = rest.astype(BF16)
    return high, middle, (rest - middle.astype(F32)).astype(BF16)


def mm(left, right):
    return jnp.dot(left, right, preferred_element_type=F32)


def mm_nt(left, right):
    return lax.dot_general(left, right, (((1,), (1,)), ((), ())), preferred_element_type=F32)


def mm_tn(left, right):
    return lax.dot_general(left, right, (((0,), (0,)), ((), ())), preferred_element_type=F32)


def iota(shape, axis):
    return lax.broadcasted_iota(jnp.int32, shape, axis)


def to_column(row):
    size = row.shape[1]
    eye = iota((size, size), 0) == iota((size, size), 1)
    return jnp.sum(jnp.where(eye, row, 0.0), axis=1, keepdims=True)


def to_row(column):
    size = column.shape[0]
    eye = iota((size, 128), 0) == iota((size, 128), 1)
    return jnp.sum(jnp.where(eye, column, 0.0), axis=0, keepdims=True)


def pair_rows(column):
    wide = jnp.broadcast_to(column, (HEADS, 128))
    head = iota((PAD, HEADS), 1)
    row = iota((PAD, HEADS), 0)
    even = jnp.dot((head == 2 * row).astype(F32), wide, precision=EXACT, preferred_element_type=F32)
    odd = jnp.dot((head == 2 * row + 1).astype(F32), wide, precision=EXACT, preferred_element_type=F32)
    return jnp.where(iota((PAD, 128), 1) < HALF, even, odd)


def unpair_sums(rows):
    first = jnp.sum(jnp.where(iota((PAD, 128), 1) < HALF, rows, 0.0), axis=1, keepdims=True)
    second = jnp.sum(jnp.where(iota((PAD, 128), 1) < HALF, 0.0, rows), axis=1, keepdims=True)
    head = iota((HEADS, PAD), 0)
    row = iota((HEADS, PAD), 1)
    first = jnp.broadcast_to(first, (PAD, 128))
    second = jnp.broadcast_to(second, (PAD, 128))
    total = jnp.dot((head == 2 * row).astype(F32), first, precision=EXACT, preferred_element_type=F32)
    total += jnp.dot((head == 2 * row + 1).astype(F32), second, precision=EXACT, preferred_element_type=F32)
    return total[:, 0:1]


def steps(logits, bias_row, decay_row):
    bias = to_column(bias_row)
    rate = -jnp.exp(to_column(decay_row))
    shifted = logits + bias
    stride = jnp.maximum(shifted, 0.0) + jnp.log1p(jnp.exp(-jnp.abs(shifted)))
    return shifted, stride, rate


def place():
    index = lax.axis_index("ctx")
    return index // (NX * NZ), (index // NZ) % NX, index % NZ


def at(y, x, z):
    return (lax.axis_index("dp"), (y * NX + x) * NZ + z)


def partner(i):
    return i + 1 - 2 * (i % 2)


def stacked(rows):
    parts = [part.astype(F32) for part in split3(rows)] + [jnp.zeros((8, LEN), F32)]
    return jnp.concatenate(parts, axis=0).T.astype(BF16)


def spread(j):
    line = iota((128, 128), 0)
    head = line - HEADS * ((line >= HEADS).astype(jnp.int32) + (line >= 2 * HEADS).astype(jnp.int32))
    return ((head == 2 * j + iota((128, 128), 1) // HALF) & (line < 3 * HEADS)).astype(BF16)


def layer_kernel(
    docs_ref,
    x_ref,
    dy_ref,
    b_ref,
    c_ref,
    logit_ref,
    bias_ref,
    decay_ref,
    skip_ref,
    mixed_ref,
    feature_ref,
    write_ref,
    read_ref,
    step_ref,
    bias_out,
    decay_out,
    skip_out,
    state_ref,
    up_in,
    up_out,
    down_in,
    down_out,
    t_out,
    x1_in,
    u2_out,
    x2_in,
    u_out,
    y1_in,
    v2_out,
    y2_in,
    zlam,
    xlam,
    ylam,
    coef,
    zsum,
    xsum,
    ysum,
    csum,
    wide_w,
    wide_f,
    y_ref,
    dx_ref,
    dg_ref,
    stack_w,
    stack_f,
    stack_l,
    stack_m,
    row_l,
    row_m,
    gram,
    gram_t,
    mask,
    mask_t,
    b_t,
    c_t,
    db,
    dc,
    rows_r,
    rows_v,
    row_last,
    row_skip,
    gains,
    lam_ref,
    send_sem,
    recv_sem,
    small_send,
    small_recv,
):
    y, x, z = place()
    core = lax.axis_index("dp")
    barrier = pltpu.get_barrier_semaphore()
    peers = [at(y, x, (z + k) % NZ) for k in range(1, NZ)]
    peers += [at(y, (x + k) % NX, z) for k in range(1, NX)]
    peers += [at((y + k) % NY, x, z) for k in range(1, NY)]
    peers += [(1 - core, lax.axis_index("ctx"))]
    for peer in peers:
        pl.semaphore_signal(barrier, inc=1, device_id=peer, device_id_type=MESH)

    def gather_copy(table, slot, target, k):
        return pltpu.make_async_remote_copy(
            src_ref=table.at[slot],
            dst_ref=table.at[slot],
            send_sem=small_send.at[k],
            recv_sem=small_recv.at[k],
            device_id=target,
            device_id_type=MESH,
        )

    def gather_start(table, own, value, targets, offset):
        table[own] = value
        for k, target in enumerate(targets):
            gather_copy(table, own, target, offset + k).start()

    def gather_end(table, own, size, targets, offset):
        for k, target in enumerate(targets):
            gather_copy(table, (own + size - 1 - k) % size, target, offset + k).wait_recv()
        for k, target in enumerate(targets):
            gather_copy(table, own, target, offset + k).wait_send()

    one = jnp.ones((PAD, 128), F32)
    zero = jnp.zeros((PAD, 128), F32)

    def products(table, own, size):
        below, above = one, one
        for k in range(size):
            below *= jnp.where(own > k, table[k], one)
            above *= jnp.where(own < k, table[k], one)
        return below, above

    shifted, stride, rate = steps(logit_ref[...], bias_ref[...], decay_ref[...])
    upper = (iota((LEN, LEN), 0) <= iota((LEN, LEN), 1)).astype(F32)
    total = jnp.dot(stride * rate, upper, precision=EXACT, preferred_element_type=F32)
    last = total[:, LEN - 1 : LEN]

    start = lax.axis_index("ctx") * LEN
    seg_row = jnp.zeros((1, LEN), jnp.int32)
    seg_col = jnp.zeros((LEN, 128), jnp.int32)
    entry = jnp.int32(0)
    final = jnp.int32(0)
    for d in range(docs_ref.shape[1]):
        doc = docs_ref[0, d] - start
        seg_row += (doc <= iota((1, LEN), 1)).astype(jnp.int32)
        seg_col += (doc <= iota((LEN, 128), 0)).astype(jnp.int32)
        entry += (doc <= -1).astype(jnp.int32)
        final += (doc <= LEN - 1).astype(jnp.int32)
    linked = (final == entry).astype(F32)
    lam_ref[...] = pair_rows(jnp.exp(last) * linked)

    pl.semaphore_wait(barrier, len(peers))
    gather_start(zlam, z, lam_ref[...], peers[:7], 0)

    seg_col = seg_col[:, 0:1]
    same = seg_col == seg_row
    mask[...] = jnp.where(same & (iota((LEN, LEN), 0) >= iota((LEN, LEN), 1)), 0.0, NEG)
    mask_t[...] = jnp.where(same & (iota((LEN, LEN), 0) <= iota((LEN, LEN), 1)), 0.0, NEG)
    keep = (seg_row == entry).astype(F32)
    own = (seg_row == final).astype(F32)
    moved = total - jnp.log(stride)
    row_l[...] = total
    row_m[...] = moved
    stack_w[...] = stacked(own * jnp.exp(last - total) * stride)
    stack_f[...] = stacked(keep * jnp.exp(total))
    stack_l[...] = stacked(total)
    stack_m[...] = stacked(moved)
    b = b_ref[...]
    c = c_ref[...]
    gram[...] = mm_nt(c, b)
    gram_t[...] = mm_nt(b, c)
    b_t[...] = b.astype(F32).T.astype(BF16)
    c_t[...] = c.astype(F32).T.astype(BF16)
    dg_ref[...] = jnp.zeros((LEN, LEN), F32)
    gains[...] = pair_rows(to_column(skip_ref[...]))
    db[...] = jnp.zeros_like(db)
    dc[...] = jnp.zeros_like(dc)
    row_last[...] = jnp.zeros_like(row_last)
    row_skip[...] = jnp.zeros_like(row_skip)

    @pl.when(z == 0)
    def _():
        up_in[...] = jnp.zeros_like(up_in)

    @pl.when(z == NZ - 1)
    def _():
        down_in[...] = jnp.zeros_like(down_in)

    gather_end(zlam, z, NZ, peers[:7], 0)
    below_z, above_z = products(zlam, z, NZ)
    coef[0, 0] = lam_ref[...]
    coef[1, 0] = lam_ref[...]
    coef[0, 1] = above_z
    coef[1, 1] = below_z
    gather_start(xlam, x, below_z * above_z * lam_ref[...], peers[7:10], 7)

    def gather_mid():
        gather_end(xlam, x, NX, peers[7:10], 7)
        below_x, above_x = products(xlam, x, NX)
        gather_start(ylam, y, below_x * above_x * xlam[x], peers[10:13], 10)

    def ring_of_four(table, own):
        mine, other = table[own], table[partner(own)]
        both = mine * other
        across = table[3 - own] * table[partner(3 - own)]
        odd = own % 2 == 1
        upper = own >= 2
        forward = (
            jnp.where(odd, one, other),
            jnp.where(odd, mine, one),
            jnp.where(odd, one, zero),
            jnp.where(upper, one, across),
            jnp.where(upper, both, one),
            jnp.where(upper, jnp.where(odd, other, one), zero),
        )
        backward = (
            jnp.where(odd, other, one),
            jnp.where(odd, one, mine),
            jnp.where(odd, zero, one),
            jnp.where(upper, across, one),
            jnp.where(upper, one, both),
            jnp.where(upper, zero, jnp.where(odd, one, other)),
        )
        return forward, backward

    def gather_last():
        gather_end(ylam, y, NY, peers[10:13], 10)
        below_x, above_x = products(xlam, x, NX)
        in_x = ring_of_four(xlam, x)
        in_y = ring_of_four(ylam, y)
        for d in range(2):
            outer = coef[1 - d, 1]
            outer_x = outer * (below_x if d == 0 else above_x)
            table = (
                in_x[d][0],
                in_x[d][1],
                in_x[d][3],
                in_x[d][4],
                in_y[d][0],
                in_y[d][1],
                outer * in_x[d][2],
                outer * in_x[d][5],
                outer_x * in_y[d][2],
                outer_x * in_y[d][5],
            )
            for k, value in enumerate(table):
                coef[d, k + 2] = value

    to_up = at(y, x, (z + 1) % NZ)
    to_down = at(y, x, (z + NZ - 1) % NZ)
    to_x1 = at(y, partner(x), z)
    to_x2 = at(y, 3 - x, z)
    to_y1 = at(partner(y), x, z)
    to_y2 = at(3 - y, x, z)

    def link(stage, c, source, target, device):
        return pltpu.make_async_remote_copy(
            src_ref=source.at[c],
            dst_ref=target.at[c],
            send_sem=send_sem.at[stage, c],
            recv_sem=recv_sem.at[stage, c],
            device_id=device,
            device_id_type=MESH,
        )

    links = (
        functools.partial(link, 0, source=up_out, target=up_in, device=to_up),
        functools.partial(link, 1, source=down_out, target=down_in, device=to_down),
        functools.partial(link, 2, source=t_out, target=x1_in, device=to_x1),
        functools.partial(link, 3, source=u2_out, target=x2_in, device=to_x2),
        functools.partial(link, 4, source=u_out, target=y1_in, device=to_y1),
        functools.partial(link, 5, source=v2_out, target=y2_in, device=to_y2),
    )

    def staged(c):
        return (c >= 0) & (c < CHUNKS)

    lag_t = HOP * jnp.maximum(z, NZ - 1 - z)
    first = iota((LEN, 128), 1) < HALF

    def row(d, k, c):
        return coef[d, k, pl.ds(c // SPLIT, 1), :]

    def begin_pair(j):
        lanes = pl.ds(pl.multiple_of(j * 128, 128), 128)
        expand = spread(j)
        w = mm(stack_w[...], expand)
        f = mm(stack_f[...], expand)
        wide_w[:, lanes] = w
        wide_f[:, lanes] = f
        high, low = split2(w * x_ref[:, lanes].astype(F32))
        state = mm(b_t[...], high) + mm(b_t[...], low)
        high, low = split2(f * dy_ref[:, lanes].astype(F32))
        state_b = mm(c_t[...], high) + mm(c_t[...], low)
        for k in range(SPLIT):
            state_ref[SPLIT * j + k, 0] = state[k * ROWS : (k + 1) * ROWS]
            state_ref[SPLIT * j + k, 1] = state_b[k * ROWS : (k + 1) * ROWS]

    def mix_head(h):
        j = h // 2
        second = h % 2 == 1
        lanes = pl.ds(pl.multiple_of(j * 128, 128), 128)
        xs = x_ref[:, lanes]
        dys = dy_ref[:, lanes]
        expand = spread(j)
        columns_l = mm(stack_l[...], expand)
        columns_m = mm(stack_m[...], expand)
        lrow = row_l[pl.ds(h, 1), :]
        mrow = row_m[pl.ds(h, 1), :]
        lcol = jnp.where(second, columns_l[:, HALF : HALF + 1], columns_l[:, 0:1])
        mcol = jnp.where(second, columns_m[:, HALF : HALF + 1], columns_m[:, 0:1])
        ours = first != second
        decays = jnp.exp((lcol - mrow) + mask[...])
        high, low = split2(decays * gram[...])
        y_ref[:, lanes] = jnp.where(ours, mm(high, xs) + mm(low, xs), y_ref[:, lanes])
        part = jnp.where(ours, dys, jnp.zeros_like(dys))
        dg_ref[...] += mm_nt(part, xs) * decays
        decays_t = jnp.exp((lrow - mcol) + mask_t[...])
        high, low = split2(decays_t * gram_t[...])
        dx_ref[:, lanes] = jnp.where(ours, mm(high, dys) + mm(low, dys), dx_ref[:, lanes])

    def finish_pair(j):
        lanes = pl.ds(pl.multiple_of(j * 128, 128), 128)
        both = []
        for d, near in ((0, up_in), (1, down_in)):
            pieces = []
            for k in range(SPLIT):
                c_end = SPLIT * j + k
                pieces.append(
                    near[c_end, d]
                    + (
                        (row(d, 8, c_end) * x1_in[c_end, d] + row(d, 9, c_end) * x2_in[c_end, d])
                        + (row(d, 10, c_end) * y1_in[c_end, d] + row(d, 11, c_end) * y2_in[c_end, d])
                    )
                )
            both.append(jnp.concatenate(pieces, axis=0))
        state_in, adjoint = both
        state_end = jnp.concatenate([state_ref[SPLIT * j + k, 0] for k in range(SPLIT)], axis=0)
        xs = x_ref[:, lanes].astype(F32)
        dys = dy_ref[:, lanes].astype(F32)
        w = wide_w[:, lanes]
        f = wide_f[:, lanes]
        gain = gains[pl.ds(j, 1), :]
        s_high, s_low = split2(state_in)
        a_high, a_low = split2(adjoint)
        inner = y_ref[:, lanes] + f * (mm(c_ref[...], s_high) + mm(c_ref[...], s_low))
        inner_t = dx_ref[:, lanes] + w * (mm(b_ref[...], a_high) + mm(b_ref[...], a_low))
        mixed_ref[:, lanes] = (inner + gain * xs).astype(BF16)
        feature_ref[:, lanes] = (inner_t + gain * dys).astype(BF16)
        select = (iota((8, 128), 1) // HALF == iota((8, 128), 0)).astype(BF16)
        high, middle, low = split3(dys * inner)
        r = mm_nt(select, high) + (mm_nt(select, middle) + mm_nt(select, low))
        high, middle, low = split3(xs * inner_t)
        v = mm_nt(select, high) + (mm_nt(select, middle) + mm_nt(select, low))
        for k in range(2):
            rows_r[pl.ds(2 * j + k, 1), :] = r[k : k + 1]
            rows_v[pl.ds(2 * j + k, 1), :] = v[k : k + 1]
        high, low = split2(f * dys)
        dc[...] += mm_nt(high, s_high) + (mm_nt(high, s_low) + mm_nt(low, s_high))
        high, low = split2(w * xs)
        db[...] += mm_nt(high, a_high) + (mm_nt(high, a_low) + mm_nt(low, a_high))
        row_skip[pl.ds(j, 1), :] = jnp.sum(dys * xs, axis=0, keepdims=True)
        leaving = lam_ref[pl.ds(j, 1), :] * state_in + state_end
        row_last[pl.ds(j, 1), :] = jnp.sum(adjoint * leaving, axis=0, keepdims=True)

    def tick(i, carry):
        @pl.when((i < CHUNKS) & (i % SPLIT == 0))
        def _():
            begin_pair(i // SPLIT)

        c_up = i - HOP * z

        @pl.when(staged(c_up))
        def _():
            @pl.when(z > 0)
            def _():
                links[0](c_up).wait_recv()

            up_out[c_up, 0] = row(0, 0, c_up) * up_in[c_up, 0] + state_ref[c_up, 0]
            up_out[c_up, 1] = up_in[c_up, 1] + row(1, 1, c_up) * state_ref[c_up, 1]

            @pl.when(z < NZ - 1)
            def _():
                links[0](c_up).start()

        c_down = i - HOP * (NZ - 1 - z)

        @pl.when(staged(c_down))
        def _():
            @pl.when(z < NZ - 1)
            def _():
                links[1](c_down).wait_recv()

            down_out[c_down, 0] = down_in[c_down, 0] + row(0, 1, c_down) * state_ref[c_down, 0]
            down_out[c_down, 1] = row(1, 0, c_down) * down_in[c_down, 1] + state_ref[c_down, 1]

            @pl.when(z > 0)
            def _():
                links[1](c_down).start()

        @pl.when(i == GATHER_X)
        def _():
            gather_mid()

        @pl.when(i == GATHER_Y)
        def _():
            gather_last()

        c_t = i - lag_t

        @pl.when(staged(c_t))
        def _():
            t_out[c_t, 0] = up_out[c_t, 0] * row(0, 1, c_t) + down_in[c_t, 0]
            t_out[c_t, 1] = down_out[c_t, 1] * row(1, 1, c_t) + up_in[c_t, 1]
            links[2](c_t).start()

        for stage, mine, came, result, k in (
            (2, t_out, x1_in, u2_out, 2),
            (3, u2_out, x2_in, u_out, 4),
            (4, u_out, y1_in, v2_out, 6),
        ):
            c = c_t - HOP * (stage - 1)

            @pl.when(staged(c))
            def _(stage=stage, mine=mine, came=came, result=result, k=k, c=c):
                links[stage](c).wait_recv()
                for d in range(2):
                    result[c, d] = row(d, k, c) * mine[c, d] + row(d, k + 1, c) * came[c, d]
                links[stage + 1](c).start()

        @pl.when(i < HEADS)
        def _():
            mix_head(i)

        c_end = c_t - HOP * 4

        @pl.when(staged(c_end) & (c_end % SPLIT == SPLIT - 1))
        def _():
            for k in range(SPLIT):
                links[5](c_end - (SPLIT - 1 - k)).wait_recv()
            finish_pair(c_end // SPLIT)

        return carry

    lax.fori_loop(0, CHUNKS + HOP * (NZ - 1 + 4), tick, 0)

    dg = dg_ref[...]
    high, low = split2(dg)
    read_ref[...] = (dc[...] + (mm(high, b_ref[...]) + mm(low, b_ref[...]))).astype(BF16)
    high, low = split2(dg.T)
    write_ref[...] = (db[...] + (mm(high, c_ref[...]) + mm(low, c_ref[...]))).astype(BF16)

    shifted, stride, rate = steps(logit_ref[...], bias_ref[...], decay_ref[...])
    v = rows_v[...]
    is_last = iota((HEADS, LEN), 1) == LEN - 1
    slope = rows_r[...] - v + jnp.where(is_last, unpair_sums(row_last[...]), 0.0)
    lower = (iota((LEN, LEN), 0) >= iota((LEN, LEN), 1)).astype(F32)
    slope = jnp.dot(slope, lower, precision=EXACT, preferred_element_type=F32)
    step = (v / stride + rate * slope) * (1.0 / (1.0 + jnp.exp(-shifted)))
    step_ref[...] = step
    bias_sum = jnp.sum(step, axis=1, keepdims=True)
    decay_sum = jnp.sum(slope * (rate * stride), axis=1, keepdims=True)
    skip_sum = unpair_sums(row_skip[...])
    sums = jnp.concatenate(
        [to_row(bias_sum), to_row(decay_sum), to_row(skip_sum), jnp.zeros((5, 128), F32)], axis=0
    )
    gather_start(csum, core, sums, peers[13:14], 13)
    gather_end(csum, core, 2, peers[13:14], 13)
    gather_start(zsum, z, csum[0] + csum[1], peers[:7], 14)
    gather_end(zsum, z, NZ, peers[:7], 14)
    gather_start(xsum, x, jnp.sum(zsum[...], axis=0), peers[7:10], 21)
    gather_end(xsum, x, NX, peers[7:10], 21)
    gather_start(ysum, y, jnp.sum(xsum[...], axis=0), peers[10:13], 24)
    gather_end(ysum, y, NY, peers[10:13], 24)
    sums = jnp.sum(ysum[...], axis=0)
    bias_out[...] = sums[0:1, :HEADS]
    decay_out[...] = sums[1:2, :HEADS]
    skip_out[...] = sums[2:3, :HEADS]

    def drain(c, carry):
        @pl.when(z < NZ - 1)
        def _():
            links[0](c).wait_send()

        @pl.when(z > 0)
        def _():
            links[1](c).wait_send()

        for stage in range(2, 6):
            links[stage](c).wait_send()
        return carry

    lax.fori_loop(0, CHUNKS, drain, 0)


VM = pl.BlockSpec(memory_space=pltpu.VMEM)
SM = pl.BlockSpec(memory_space=pltpu.SMEM)


def shape(dims, kind=F32):
    return jax.ShapeDtypeStruct(dims, kind)


def local(
    features,
    write_keys,
    read_queries,
    step_logits,
    step_bias,
    decay_log,
    skip_gain,
    doc_starts,
    out_grad,
):
    x, b, c, logits, dy = features[0], write_keys[0], read_queries[0], step_logits[0], out_grad[0]
    bias, decay, skip = step_bias[None], decay_log[None], skip_gain[None]
    carry_shape = (CHUNKS, 2, ROWS, 128)
    outputs = pl.pallas_call(
        layer_kernel,
        out_shape=(
            shape((LEN, WIDE), BF16),
            shape((LEN, WIDE), BF16),
            shape((LEN, 128), BF16),
            shape((LEN, 128), BF16),
            shape((HEADS, LEN)),
            shape((1, HEADS)),
            shape((1, HEADS)),
            shape((1, HEADS)),
        ),
        in_specs=[SM] + [VM] * 8,
        out_specs=(VM,) * 8,
        scratch_shapes=[pltpu.VMEM(carry_shape, F32)] * 13
        + [pltpu.VMEM((n, PAD, 128), F32) for n in (NZ, NX, NY)]
        + [pltpu.VMEM((2, 12, PAD, 128), F32)]
        + [pltpu.VMEM((n, 8, 128), F32) for n in (NZ, NX, NY, 2)]
        + [pltpu.VMEM((LEN, WIDE), F32)] * 4
        + [pltpu.VMEM((LEN, LEN), F32)]
        + [pltpu.VMEM((LEN, 128), BF16)] * 4
        + [pltpu.VMEM((HEADS, LEN), F32)] * 2
        + [pltpu.VMEM((LEN, LEN), F32)] * 4
        + [pltpu.VMEM((128, LEN), BF16)] * 2
        + [pltpu.VMEM((LEN, 128), F32)] * 2
        + [pltpu.VMEM((HEADS, LEN), F32)] * 2
        + [pltpu.VMEM((PAD, 128), F32)] * 4
        + [pltpu.SemaphoreType.DMA((6, CHUNKS))] * 2
        + [pltpu.SemaphoreType.DMA((27,))] * 2,
        compiler_params=pltpu.CompilerParams(
            collective_id=0, has_side_effects=True, vmem_limit_bytes=60 * 2**20
        ),
        name="layer",
    )(doc_starts, x, dy, b, c, logits, bias, decay, skip)
    mixed, feature_grad, write_grad, read_grad, step_grad, bias_sum, decay_sum, skip_sum = outputs
    return (
        mixed[None],
        feature_grad[None],
        write_grad[None],
        read_grad[None],
        step_grad[None],
        bias_sum[0],
        decay_sum[0],
        skip_sum[0],
    )


def solution(mesh):
    in_specs = (
        P("dp", "ctx", None),
        P("dp", "ctx", None),
        P("dp", "ctx", None),
        P("dp", None, "ctx"),
        P(),
        P(),
        P(),
        P("dp", None),
        P("dp", "ctx", None),
    )
    out_specs = (
        P("dp", "ctx", None),
        P("dp", "ctx", None),
        P("dp", "ctx", None),
        P("dp", "ctx", None),
        P("dp", None, "ctx"),
        P(),
        P(),
        P(),
    )
    return jax.shard_map(local, mesh=mesh, in_specs=in_specs, out_specs=out_specs, check_vma=False)
```

```python
import functools

import jax
import jax.numpy as jnp
from jax import lax
from jax.experimental import pallas as pl
from jax.experimental.pallas import tpu as pltpu
from jax.sharding import PartitionSpec as P

MESH = pl.DeviceIdType.MESH
F32 = jnp.float32
BF16 = jnp.bfloat16
EXACT = lax.Precision.HIGHEST

HEADS = 40
PAIRS = 20
PAD = 24
HALF = 64
LEN = 256
WIDE = 2560
CHUNKS = 40
SPLIT = CHUNKS // PAIRS
ROWS = 128 // SPLIT
NY, NX, NZ = 4, 4, 8
HOP = 3
GATHER_Z = HOP - 1
GATHER_X = 2 * HOP - 1
GATHER_Y = 3 * HOP - 1
LATER = HOP
SET = CHUNKS // 2
NEG = -1e30


def split2(value):
    high = value.astype(BF16)
    return high, (value - high.astype(F32)).astype(BF16)


def split3(value):
    high = value.astype(BF16)
    rest = value - high.astype(F32)
    middle = rest.astype(BF16)
    return high, middle, (rest - middle.astype(F32)).astype(BF16)


def mm(left, right):
    return jnp.dot(left, right, preferred_element_type=F32)


def mm_nt(left, right):
    return lax.dot_general(left, right, (((1,), (1,)), ((), ())), preferred_element_type=F32)


def mm_tn(left, right):
    return lax.dot_general(left, right, (((0,), (0,)), ((), ())), preferred_element_type=F32)


def iota(shape, axis):
    return lax.broadcasted_iota(jnp.int32, shape, axis)


def to_column(row):
    size = row.shape[1]
    eye = iota((size, size), 0) == iota((size, size), 1)
    return jnp.sum(jnp.where(eye, row, 0.0), axis=1, keepdims=True)


def to_row(column):
    size = column.shape[0]
    eye = iota((size, 128), 0) == iota((size, 128), 1)
    return jnp.sum(jnp.where(eye, column, 0.0), axis=0, keepdims=True)


def pair_rows(column):
    wide = jnp.broadcast_to(column, (HEADS, 128))
    head = iota((PAD, HEADS), 1)
    row = iota((PAD, HEADS), 0)
    even = jnp.dot((head == 2 * row).astype(F32), wide, precision=EXACT, preferred_element_type=F32)
    odd = jnp.dot((head == 2 * row + 1).astype(F32), wide, precision=EXACT, preferred_element_type=F32)
    return jnp.where(iota((PAD, 128), 1) < HALF, even, odd)


def unpair_sums(rows):
    first = jnp.sum(jnp.where(iota((PAD, 128), 1) < HALF, rows, 0.0), axis=1, keepdims=True)
    second = jnp.sum(jnp.where(iota((PAD, 128), 1) < HALF, 0.0, rows), axis=1, keepdims=True)
    head = iota((HEADS, PAD), 0)
    row = iota((HEADS, PAD), 1)
    first = jnp.broadcast_to(first, (PAD, 128))
    second = jnp.broadcast_to(second, (PAD, 128))
    total = jnp.dot((head == 2 * row).astype(F32), first, precision=EXACT, preferred_element_type=F32)
    total += jnp.dot((head == 2 * row + 1).astype(F32), second, precision=EXACT, preferred_element_type=F32)
    return total[:, 0:1]


def steps(logits, bias_row, decay_row):
    bias = to_column(bias_row)
    rate = -jnp.exp(to_column(decay_row))
    shifted = logits + bias
    stride = jnp.maximum(shifted, 0.0) + jnp.log1p(jnp.exp(-jnp.abs(shifted)))
    return shifted, stride, rate


def place():
    index = lax.axis_index("ctx")
    return index // (NX * NZ), (index // NZ) % NX, index % NZ


def at(y, x, z):
    return (lax.axis_index("dp"), (y * NX + x) * NZ + z)


def partner(i):
    return i + 1 - 2 * (i % 2)


def stacked(rows):
    parts = [part.astype(F32) for part in split3(rows)] + [jnp.zeros((8, LEN), F32)]
    return jnp.concatenate(parts, axis=0).T.astype(BF16)


def spread(j):
    line = iota((128, 128), 0)
    head = line - HEADS * ((line >= HEADS).astype(jnp.int32) + (line >= 2 * HEADS).astype(jnp.int32))
    return ((head == 2 * j + iota((128, 128), 1) // HALF) & (line < 3 * HEADS)).astype(BF16)


def layer_kernel(
    docs_ref,
    x_ref,
    dy_ref,
    b_ref,
    c_ref,
    logit_ref,
    bias_ref,
    decay_ref,
    skip_ref,
    mixed_ref,
    feature_ref,
    write_ref,
    read_ref,
    step_ref,
    bias_out,
    decay_out,
    skip_out,
    state_ref,
    up_in,
    up_out,
    down_in,
    down_out,
    t_out,
    x1_in,
    u2_out,
    x2_in,
    u_out,
    y1_in,
    v2_out,
    y2_in,
    f_buf,
    entering,
    zlam,
    xlam,
    ylam,
    coef,
    column_sums,
    plane_sums,
    wide_w,
    wide_f,
    y_ref,
    dx_ref,
    dg_ref,
    stack_w,
    stack_f,
    stack_l,
    stack_m,
    row_l,
    row_m,
    gram,
    gram_t,
    mask,
    mask_t,
    b_t,
    c_t,
    db,
    dc,
    rows_r,
    rows_v,
    row_last,
    row_skip,
    gains,
    lam_ref,
    send_sem,
    recv_sem,
    small_send,
    small_recv,
):
    y, x, z = place()
    core = lax.axis_index("dp")
    barrier = pltpu.get_barrier_semaphore()
    along_z = [at(y, x, (z + k) % NZ) for k in range(1, NZ)]
    along_x = [at(y, (x + k) % NX, z) for k in range(1, NX)]
    along_y = [at((y + k) % NY, x, z) for k in range(1, NY)]
    column = core * NZ + z
    cell = y * NX + x
    in_column = []
    for k in range(1, 2 * NZ):
        other = (column + k) % (2 * NZ)
        in_column.append((other // NZ, cell * NZ + other % NZ))
    in_plane = []
    for k in range(1, NX * NY):
        other = (cell + k) % (NX * NY)
        in_plane.append((core, other * NZ + z))
    peers = in_column + in_plane
    for peer in peers:
        pl.semaphore_signal(barrier, inc=1, device_id=peer, device_id_type=MESH)

    def gather_copy(table, slot, target, k):
        return pltpu.make_async_remote_copy(
            src_ref=table.at[slot],
            dst_ref=table.at[slot],
            send_sem=small_send.at[k],
            recv_sem=small_recv.at[k],
            device_id=target,
            device_id_type=MESH,
        )

    def gather_start(table, own, value, targets, offset):
        table[own] = value
        for k, target in enumerate(targets):
            gather_copy(table, own, target, offset + k).start()

    def gather_end(table, own, size, targets, offset):
        for k, target in enumerate(targets):
            gather_copy(table, (own + size - 1 - k) % size, target, offset + k).wait_recv()
        for k, target in enumerate(targets):
            gather_copy(table, own, target, offset + k).wait_send()

    one = jnp.ones((PAD, 128), F32)
    zero = jnp.zeros((PAD, 128), F32)

    def products(table, own, size):
        below, above = one, one
        for k in range(size):
            below *= jnp.where(own > k, table[k], one)
            above *= jnp.where(own < k, table[k], one)
        return below, above

    shifted, stride, rate = steps(logit_ref[...], bias_ref[...], decay_ref[...])
    upper = (iota((LEN, LEN), 0) <= iota((LEN, LEN), 1)).astype(F32)
    total = jnp.dot(stride * rate, upper, precision=EXACT, preferred_element_type=F32)
    last = total[:, LEN - 1 : LEN]

    start = lax.axis_index("ctx") * LEN
    seg_row = jnp.zeros((1, LEN), jnp.int32)
    seg_col = jnp.zeros((LEN, 128), jnp.int32)
    entry = jnp.int32(0)
    final = jnp.int32(0)
    for d in range(docs_ref.shape[1]):
        doc = docs_ref[0, d] - start
        seg_row += (doc <= iota((1, LEN), 1)).astype(jnp.int32)
        seg_col += (doc <= iota((LEN, 128), 0)).astype(jnp.int32)
        entry += (doc <= -1).astype(jnp.int32)
        final += (doc <= LEN - 1).astype(jnp.int32)
    linked = (final == entry).astype(F32)
    lam_ref[...] = pair_rows(jnp.exp(last) * linked)

    pl.semaphore_wait(barrier, len(peers))
    gather_start(zlam, z, lam_ref[...], along_z, 0)

    seg_col = seg_col[:, 0:1]
    same = seg_col == seg_row
    mask[...] = jnp.where(same & (iota((LEN, LEN), 0) >= iota((LEN, LEN), 1)), 0.0, NEG)
    mask_t[...] = jnp.where(same & (iota((LEN, LEN), 0) <= iota((LEN, LEN), 1)), 0.0, NEG)
    keep = (seg_row == entry).astype(F32)
    own = (seg_row == final).astype(F32)
    moved = total - jnp.log(stride)
    row_l[...] = total
    row_m[...] = moved
    stack_w[...] = stacked(own * jnp.exp(last - total) * stride)
    stack_f[...] = stacked(keep * jnp.exp(total))
    stack_l[...] = stacked(total)
    stack_m[...] = stacked(moved)
    b = b_ref[...]
    c = c_ref[...]
    gram[...] = mm_nt(c, b)
    gram_t[...] = mm_nt(b, c)
    b_t[...] = b.astype(F32).T.astype(BF16)
    c_t[...] = c.astype(F32).T.astype(BF16)
    dg_ref[...] = jnp.zeros((LEN, LEN), F32)
    gains[...] = pair_rows(to_column(skip_ref[...]))
    db[...] = jnp.zeros_like(db)
    dc[...] = jnp.zeros_like(dc)
    row_last[...] = jnp.zeros_like(row_last)
    row_skip[...] = jnp.zeros_like(row_skip)

    @pl.when(z == 0)
    def _():
        up_in[...] = jnp.zeros_like(up_in)

    @pl.when(z == NZ - 1)
    def _():
        down_in[...] = jnp.zeros_like(down_in)

    for d in range(2):
        coef[d, 0] = lam_ref[...]
        coef[d, 1] = one

    def gather_first():
        gather_end(zlam, z, NZ, along_z, 0)
        below_z, above_z = products(zlam, z, NZ)
        coef[0, 1] = above_z
        coef[1, 1] = below_z
        gather_start(xlam, x, below_z * above_z * lam_ref[...], along_x, 7)

    def ring_of_four(table, own):
        mine, other = table[own], table[partner(own)]
        both = mine * other
        across = table[3 - own] * table[partner(3 - own)]
        odd = own % 2 == 1
        upper = own >= 2
        forward = (
            jnp.where(odd, one, other),
            jnp.where(odd, mine, one),
            jnp.where(odd, one, zero),
            jnp.where(upper, one, across),
            jnp.where(upper, both, one),
            jnp.where(upper, jnp.where(odd, other, one), zero),
        )
        backward = (
            jnp.where(odd, other, one),
            jnp.where(odd, one, mine),
            jnp.where(odd, zero, one),
            jnp.where(upper, across, one),
            jnp.where(upper, one, both),
            jnp.where(upper, zero, jnp.where(odd, one, other)),
        )
        return forward, backward

    def put(d, k, values):
        for value in values:
            coef[d, k] = value
            k += 1

    def gather_mid():
        gather_end(xlam, x, NX, along_x, 7)
        below_x, above_x = products(xlam, x, NX)
        gather_start(ylam, y, below_x * above_x * xlam[x], along_y, 10)
        in_x = ring_of_four(xlam, x)
        for d in range(2):
            put(d, 2, (in_x[d][0], in_x[d][1], in_x[d][3], in_x[d][4]))
            put(d, 8, (in_x[d][2], in_x[d][5]))

    def gather_last():
        gather_end(ylam, y, NY, along_y, 10)
        below_x, above_x = products(xlam, x, NX)
        in_y = ring_of_four(ylam, y)
        for d in range(2):
            outer_x = below_x if d == 0 else above_x
            put(d, 6, (in_y[d][0], in_y[d][1]))
            put(d, 10, (outer_x * in_y[d][2], outer_x * in_y[d][5]))

    to_up = at(y, x, (z + 1) % NZ)
    to_down = at(y, x, (z + NZ - 1) % NZ)
    to_x1 = at(y, partner(x), z)
    to_x2 = at(y, 3 - x, z)
    to_y1 = at(partner(y), x, z)
    to_y2 = at(3 - y, x, z)

    def link(stage, c, source, target, device):
        return pltpu.make_async_remote_copy(
            src_ref=source.at[c],
            dst_ref=target.at[c],
            send_sem=send_sem.at[stage, c],
            recv_sem=recv_sem.at[stage, c],
            device_id=device,
            device_id_type=MESH,
        )

    links = (
        functools.partial(link, 0, source=up_out, target=up_in, device=to_up),
        functools.partial(link, 1, source=down_out, target=down_in, device=to_down),
        functools.partial(link, 2, source=t_out, target=x1_in, device=to_x1),
        functools.partial(link, 3, source=u2_out, target=x2_in, device=to_x2),
        functools.partial(link, 4, source=u_out, target=y1_in, device=to_y1),
        functools.partial(link, 5, source=v2_out, target=y2_in, device=to_y2),
    )

    def staged(n):
        return (n >= 0) & (n < SET)

    def chunk(n, second):
        return 4 * (n // 2) + n % 2 + 2 * second

    def outside(c, d):
        return (row(d, 8, c) * x1_in[c, d] + row(d, 9, c) * x2_in[c, d]) + (
            row(d, 10, c) * y1_in[c, d] + row(d, 11, c) * y2_in[c, d]
        )

    lag_t = HOP * jnp.maximum(z, NZ - 1 - z)
    first = iota((LEN, 128), 1) < HALF

    def row(d, k, c):
        return coef[d, k, pl.ds(c // SPLIT, 1), :]

    def begin_pair(j):
        lanes = pl.ds(pl.multiple_of(j * 128, 128), 128)
        expand = spread(j)
        w = mm(stack_w[...], expand)
        f = mm(stack_f[...], expand)
        wide_w[:, lanes] = w
        wide_f[:, lanes] = f
        high, low = split2(w * x_ref[:, lanes].astype(F32))
        state = mm(b_t[...], high) + mm(b_t[...], low)
        high, low = split2(f * dy_ref[:, lanes].astype(F32))
        state_b = mm(c_t[...], high) + mm(c_t[...], low)
        for k in range(SPLIT):
            state_ref[SPLIT * j + k, 0] = state[k * ROWS : (k + 1) * ROWS]
            state_ref[SPLIT * j + k, 1] = state_b[k * ROWS : (k + 1) * ROWS]

    def mix_head(h):
        j = h // 2
        second = h % 2 == 1
        lanes = pl.ds(pl.multiple_of(j * 128, 128), 128)
        xs = x_ref[:, lanes]
        dys = dy_ref[:, lanes]
        expand = spread(j)
        columns_l = mm(stack_l[...], expand)
        columns_m = mm(stack_m[...], expand)
        lrow = row_l[pl.ds(h, 1), :]
        mrow = row_m[pl.ds(h, 1), :]
        lcol = jnp.where(second, columns_l[:, HALF : HALF + 1], columns_l[:, 0:1])
        mcol = jnp.where(second, columns_m[:, HALF : HALF + 1], columns_m[:, 0:1])
        ours = first != second
        decays = jnp.exp((lcol - mrow) + mask[...])
        high, low = split2(decays * gram[...])
        y_ref[:, lanes] = jnp.where(ours, mm(high, xs) + mm(low, xs), y_ref[:, lanes])
        part = jnp.where(ours, dys, jnp.zeros_like(dys))
        dg_ref[...] += mm_nt(part, xs) * decays
        decays_t = jnp.exp((lrow - mcol) + mask_t[...])
        high, low = split2(decays_t * gram_t[...])
        dx_ref[:, lanes] = jnp.where(ours, mm(high, dys) + mm(low, dys), dx_ref[:, lanes])

    def finish_pair(j):
        lanes = pl.ds(pl.multiple_of(j * 128, 128), 128)
        state_in, adjoint = entering[0], entering[1]
        state_end = jnp.concatenate([state_ref[SPLIT * j + k, 0] for k in range(SPLIT)], axis=0)
        xs = x_ref[:, lanes].astype(F32)
        dys = dy_ref[:, lanes].astype(F32)
        w = wide_w[:, lanes]
        f = wide_f[:, lanes]
        gain = gains[pl.ds(j, 1), :]
        s_high, s_low = split2(state_in)
        a_high, a_low = split2(adjoint)
        inner = y_ref[:, lanes] + f * (mm(c_ref[...], s_high) + mm(c_ref[...], s_low))
        inner_t = dx_ref[:, lanes] + w * (mm(b_ref[...], a_high) + mm(b_ref[...], a_low))
        mixed_ref[:, lanes] = (inner + gain * xs).astype(BF16)
        feature_ref[:, lanes] = (inner_t + gain * dys).astype(BF16)
        select = (iota((8, 128), 1) // HALF == iota((8, 128), 0)).astype(BF16)
        high, middle, low = split3(dys * inner)
        r = mm_nt(select, high) + (mm_nt(select, middle) + mm_nt(select, low))
        high, middle, low = split3(xs * inner_t)
        v = mm_nt(select, high) + (mm_nt(select, middle) + mm_nt(select, low))
        for k in range(2):
            rows_r[pl.ds(2 * j + k, 1), :] = r[k : k + 1]
            rows_v[pl.ds(2 * j + k, 1), :] = v[k : k + 1]
        high, low = split2(f * dys)
        dc[...] += mm_nt(high, s_high) + (mm_nt(high, s_low) + mm_nt(low, s_high))
        high, low = split2(w * xs)
        db[...] += mm_nt(high, a_high) + (mm_nt(high, a_low) + mm_nt(low, a_high))
        row_skip[pl.ds(j, 1), :] = jnp.sum(dys * xs, axis=0, keepdims=True)
        leaving = lam_ref[pl.ds(j, 1), :] * state_in + state_end
        row_last[pl.ds(j, 1), :] = jnp.sum(adjoint * leaving, axis=0, keepdims=True)

    def tick(i, carry):
        @pl.when(i == GATHER_Z)
        def _():
            gather_first()

        @pl.when(i == GATHER_X)
        def _():
            gather_mid()

        @pl.when(i == GATHER_Y)
        def _():
            gather_last()

        @pl.when(i < PAIRS)
        def _():
            begin_pair(i)

        def chains(second):
            since = i - (LATER + 4 * HOP) * second
            n = since - HOP * z

            @pl.when(staged(n))
            def _(second=second, n=n):
                c = chunk(n, second)

                @pl.when(z > 0)
                def _():
                    links[0](c).wait_recv()

                if second:
                    ahead = up_in[c, 0] + row(1, 1, c) * f_buf[c, 0]
                    up_out[c, 0] = row(0, 0, c) * ahead + state_ref[c, 0]
                    up_out[c, 1] = up_in[c, 1] + f_buf[c, 1]
                else:
                    up_out[c, 0] = row(0, 0, c) * up_in[c, 0] + state_ref[c, 0]
                    up_out[c, 1] = up_in[c, 1] + row(1, 1, c) * state_ref[c, 1]

                @pl.when(z < NZ - 1)
                def _():
                    links[0](c).start()

            n = since - HOP * (NZ - 1 - z)

            @pl.when(staged(n))
            def _(second=second, n=n):
                c = chunk(n, second)

                @pl.when(z < NZ - 1)
                def _():
                    links[1](c).wait_recv()

                if second:
                    ahead = down_in[c, 1] + row(0, 1, c) * f_buf[c, 1]
                    down_out[c, 0] = down_in[c, 0] + f_buf[c, 0]
                    down_out[c, 1] = row(1, 0, c) * ahead + state_ref[c, 1]
                else:
                    down_out[c, 0] = down_in[c, 0] + row(0, 1, c) * state_ref[c, 0]
                    down_out[c, 1] = row(1, 0, c) * down_in[c, 1] + state_ref[c, 1]

                @pl.when(z > 0)
                def _():
                    links[1](c).start()

        def exchanges(second):
            first_at = i - LATER if second else i - lag_t

            @pl.when(staged(first_at))
            def _(second=second, first_at=first_at):
                c = chunk(first_at, second)
                if second:
                    t_out[c, 0] = row(0, 1, c) * state_ref[c, 0]
                    t_out[c, 1] = row(1, 1, c) * state_ref[c, 1]
                else:
                    t_out[c, 0] = up_out[c, 0] * row(0, 1, c) + down_in[c, 0]
                    t_out[c, 1] = down_out[c, 1] * row(1, 1, c) + up_in[c, 1]
                links[2](c).start()

            for stage, mine, came, result, k in (
                (2, t_out, x1_in, u2_out, 2),
                (3, u2_out, x2_in, u_out, 4),
                (4, u_out, y1_in, v2_out, 6),
            ):
                n = first_at - HOP * (stage - 1)

                @pl.when(staged(n))
                def _(stage=stage, mine=mine, came=came, result=result, k=k, n=n, second=second):
                    c = chunk(n, second)
                    links[stage](c).wait_recv()
                    for d in range(2):
                        result[c, d] = row(d, k, c) * mine[c, d] + row(d, k + 1, c) * came[c, d]
                    links[stage + 1](c).start()

            n = first_at - HOP * 4

            @pl.when(staged(n))
            def _(second=second, n=n):
                c = chunk(n, second)
                links[5](c).wait_recv()
                for d in range(2):
                    f_buf[c, d] = outside(c, d)

        exchanges(1)
        chains(0)
        chains(1)
        exchanges(0)

        @pl.when(i < HEADS)
        def _():
            mix_head(i)

        for second in (0, 1):
            n = i - lag_t - HOP * 4 - LATER * second

            @pl.when(staged(n) & (n % 2 == 1))
            def _(second=second, n=n):
                for k in range(2):
                    c = chunk(n - 1 + k, second)
                    lines = slice(k * ROWS, (k + 1) * ROWS)
                    if second:
                        entering[0, lines] = up_in[c, 0] + row(1, 1, c) * (down_in[c, 0] + f_buf[c, 0])
                        entering[1, lines] = down_in[c, 1] + row(0, 1, c) * (up_in[c, 1] + f_buf[c, 1])
                    else:
                        entering[0, lines] = up_in[c, 0] + row(1, 1, c) * f_buf[c, 0]
                        entering[1, lines] = down_in[c, 1] + row(0, 1, c) * f_buf[c, 1]

        done_at = i - lag_t - HOP * 4
        second = 1 - done_at % 2
        n = done_at - LATER * second

        @pl.when(staged(n))
        def _():
            finish_pair(2 * (n // 2) + second)

        return carry

    lax.fori_loop(0, SET + HOP * (NZ - 1 + 4) + LATER, tick, 0)

    dg = dg_ref[...]
    high, low = split2(dg)
    read_ref[...] = (dc[...] + (mm(high, b_ref[...]) + mm(low, b_ref[...]))).astype(BF16)
    high, low = split2(dg.T)
    write_ref[...] = (db[...] + (mm(high, c_ref[...]) + mm(low, c_ref[...]))).astype(BF16)

    shifted, stride, rate = steps(logit_ref[...], bias_ref[...], decay_ref[...])
    v = rows_v[...]
    is_last = iota((HEADS, LEN), 1) == LEN - 1
    slope = rows_r[...] - v + jnp.where(is_last, unpair_sums(row_last[...]), 0.0)
    lower = (iota((LEN, LEN), 0) >= iota((LEN, LEN), 1)).astype(F32)
    slope = jnp.dot(slope, lower, precision=EXACT, preferred_element_type=F32)
    step = (v / stride + rate * slope) * (1.0 / (1.0 + jnp.exp(-shifted)))
    step_ref[...] = step
    bias_sum = jnp.sum(step, axis=1, keepdims=True)
    decay_sum = jnp.sum(slope * (rate * stride), axis=1, keepdims=True)
    skip_sum = unpair_sums(row_skip[...])
    sums = jnp.concatenate(
        [to_row(bias_sum), to_row(decay_sum), to_row(skip_sum), jnp.zeros((5, 128), F32)], axis=0
    )
    gather_start(column_sums, column, sums, in_column, 13)
    gather_end(column_sums, column, 2 * NZ, in_column, 13)
    gather_start(plane_sums, cell, jnp.sum(column_sums[...], axis=0), in_plane, 28)
    gather_end(plane_sums, cell, NX * NY, in_plane, 28)
    sums = jnp.sum(plane_sums[...], axis=0)
    bias_out[...] = sums[0:1, :HEADS]
    decay_out[...] = sums[1:2, :HEADS]
    skip_out[...] = sums[2:3, :HEADS]

    def drain(c, carry):
        @pl.when(z < NZ - 1)
        def _():
            links[0](c).wait_send()

        @pl.when(z > 0)
        def _():
            links[1](c).wait_send()

        for stage in range(2, 6):
            links[stage](c).wait_send()
        return carry

    lax.fori_loop(0, CHUNKS, drain, 0)


def emit_kernel(*refs):
    count = len(refs) // 2
    for k in range(count):
        refs[count + k][...] = refs[k][...]


VM = pl.BlockSpec(memory_space=pltpu.VMEM)
SM = pl.BlockSpec(memory_space=pltpu.SMEM)


def shape(dims, kind=F32):
    return jax.ShapeDtypeStruct(dims, kind)


def local(
    features,
    write_keys,
    read_queries,
    step_logits,
    step_bias,
    decay_log,
    skip_gain,
    doc_starts,
    out_grad,
):
    x, b, c, logits, dy = features[0], write_keys[0], read_queries[0], step_logits[0], out_grad[0]
    bias, decay, skip = step_bias[None], decay_log[None], skip_gain[None]
    carry_shape = (CHUNKS, 2, ROWS, 128)
    outputs = pl.pallas_call(
        layer_kernel,
        out_shape=(
            shape((LEN, WIDE), BF16),
            shape((LEN, WIDE), BF16),
            shape((LEN, 128), BF16),
            shape((LEN, 128), BF16),
            shape((HEADS, LEN)),
            shape((1, HEADS)),
            shape((1, HEADS)),
            shape((1, HEADS)),
        ),
        in_specs=[SM] + [VM] * 8,
        out_specs=(VM,) * 8,
        scratch_shapes=[pltpu.VMEM(carry_shape, F32)] * 14
        + [pltpu.VMEM((2, 128, 128), F32)]
        + [pltpu.VMEM((n, PAD, 128), F32) for n in (NZ, NX, NY)]
        + [pltpu.VMEM((2, 12, PAD, 128), F32)]
        + [pltpu.VMEM((n, 8, 128), F32) for n in (2 * NZ, NX * NY)]
        + [pltpu.VMEM((LEN, WIDE), F32)] * 4
        + [pltpu.VMEM((LEN, LEN), F32)]
        + [pltpu.VMEM((LEN, 128), BF16)] * 4
        + [pltpu.VMEM((HEADS, LEN), F32)] * 2
        + [pltpu.VMEM((LEN, LEN), F32)] * 4
        + [pltpu.VMEM((128, LEN), BF16)] * 2
        + [pltpu.VMEM((LEN, 128), F32)] * 2
        + [pltpu.VMEM((HEADS, LEN), F32)] * 2
        + [pltpu.VMEM((PAD, 128), F32)] * 4
        + [pltpu.SemaphoreType.DMA((6, CHUNKS))] * 2
        + [pltpu.SemaphoreType.DMA((43,))] * 2,
        compiler_params=pltpu.CompilerParams(
            collective_id=0, has_side_effects=True, vmem_limit_bytes=60 * 2**20
        ),
        name="layer",
    )(doc_starts, x, dy, b, c, logits, bias, decay, skip)
    outputs = pl.pallas_call(
        emit_kernel,
        out_shape=tuple(shape(o.shape, o.dtype) for o in outputs),
        in_specs=[VM] * 8,
        out_specs=(VM,) * 8,
        name="emit",
    )(*outputs)
    mixed, feature_grad, write_grad, read_grad, step_grad, bias_sum, decay_sum, skip_sum = outputs
    return (
        mixed[None],
        feature_grad[None],
        write_grad[None],
        read_grad[None],
        step_grad[None],
        bias_sum[0],
        decay_sum[0],
        skip_sum[0],
    )


def solution(mesh):
    in_specs = (
        P("dp", "ctx", None),
        P("dp", "ctx", None),
        P("dp", "ctx", None),
        P("dp", None, "ctx"),
        P(),
        P(),
        P(),
        P("dp", None),
        P("dp", "ctx", None),
    )
    out_specs = (
        P("dp", "ctx", None),
        P("dp", "ctx", None),
        P("dp", "ctx", None),
        P("dp", "ctx", None),
        P("dp", None, "ctx"),
        P(),
        P(),
        P(),
    )
    return jax.shard_map(local, mesh=mesh, in_specs=in_specs, out_specs=out_specs, check_vma=False)
```

```python
import functools

import jax
import jax.numpy as jnp
from jax import lax
from jax.experimental import pallas as pl
from jax.experimental.pallas import tpu as pltpu
from jax.sharding import PartitionSpec as P

MESH = pl.DeviceIdType.MESH
F32 = jnp.float32
BF16 = jnp.bfloat16
EXACT = lax.Precision.HIGHEST

HEADS = 40
PAIRS = 20
PAD = 24
HALF = 64
LEN = 256
WIDE = 2560
CHUNKS = 40
SPLIT = CHUNKS // PAIRS
ROWS = 128 // SPLIT
NY, NX, NZ = 4, 4, 8
HOP = 3
GATHER_Z = HOP - 1
GATHER_X = 2 * HOP - 1
GATHER_Y = 3 * HOP - 1
LATER = HOP
SET = CHUNKS // 2
NEG = -1e30


def split2(value):
    high = value.astype(BF16)
    return high, (value - high.astype(F32)).astype(BF16)


def split3(value):
    high = value.astype(BF16)
    rest = value - high.astype(F32)
    middle = rest.astype(BF16)
    return high, middle, (rest - middle.astype(F32)).astype(BF16)


def mm(left, right):
    return jnp.dot(left, right, preferred_element_type=F32)


def mm_nt(left, right):
    return lax.dot_general(left, right, (((1,), (1,)), ((), ())), preferred_element_type=F32)


def mm_tn(left, right):
    return lax.dot_general(left, right, (((0,), (0,)), ((), ())), preferred_element_type=F32)


def iota(shape, axis):
    return lax.broadcasted_iota(jnp.int32, shape, axis)


def to_column(row):
    size = row.shape[1]
    eye = iota((size, size), 0) == iota((size, size), 1)
    return jnp.sum(jnp.where(eye, row, 0.0), axis=1, keepdims=True)


def to_row(column):
    size = column.shape[0]
    eye = iota((size, 128), 0) == iota((size, 128), 1)
    return jnp.sum(jnp.where(eye, column, 0.0), axis=0, keepdims=True)


def pair_rows(column):
    wide = jnp.broadcast_to(column, (HEADS, 128))
    head = iota((PAD, HEADS), 1)
    row = iota((PAD, HEADS), 0)
    even = jnp.dot((head == 2 * row).astype(F32), wide, precision=EXACT, preferred_element_type=F32)
    odd = jnp.dot((head == 2 * row + 1).astype(F32), wide, precision=EXACT, preferred_element_type=F32)
    return jnp.where(iota((PAD, 128), 1) < HALF, even, odd)


def unpair_sums(rows):
    first = jnp.sum(jnp.where(iota((PAD, 128), 1) < HALF, rows, 0.0), axis=1, keepdims=True)
    second = jnp.sum(jnp.where(iota((PAD, 128), 1) < HALF, 0.0, rows), axis=1, keepdims=True)
    head = iota((HEADS, PAD), 0)
    row = iota((HEADS, PAD), 1)
    first = jnp.broadcast_to(first, (PAD, 128))
    second = jnp.broadcast_to(second, (PAD, 128))
    total = jnp.dot((head == 2 * row).astype(F32), first, precision=EXACT, preferred_element_type=F32)
    total += jnp.dot((head == 2 * row + 1).astype(F32), second, precision=EXACT, preferred_element_type=F32)
    return total[:, 0:1]


def steps(logits, bias_row, decay_row):
    bias = to_column(bias_row)
    rate = -jnp.exp(to_column(decay_row))
    shifted = logits + bias
    stride = jnp.maximum(shifted, 0.0) + jnp.log1p(jnp.exp(-jnp.abs(shifted)))
    return shifted, stride, rate


def place():
    index = lax.axis_index("ctx")
    return index // (NX * NZ), (index // NZ) % NX, index % NZ


def at(y, x, z):
    return (lax.axis_index("dp"), (y * NX + x) * NZ + z)


def partner(i):
    return i + 1 - 2 * (i % 2)


def stacked(rows):
    parts = [part.astype(F32) for part in split3(rows)] + [jnp.zeros((8, LEN), F32)]
    return jnp.concatenate(parts, axis=0).T.astype(BF16)


def spread(j):
    line = iota((128, 128), 0)
    head = line - HEADS * ((line >= HEADS).astype(jnp.int32) + (line >= 2 * HEADS).astype(jnp.int32))
    return ((head == 2 * j + iota((128, 128), 1) // HALF) & (line < 3 * HEADS)).astype(BF16)


def layer_kernel(
    docs_ref,
    x_ref,
    dy_ref,
    b_ref,
    c_ref,
    logit_ref,
    bias_ref,
    decay_ref,
    skip_ref,
    mixed_ref,
    feature_ref,
    write_ref,
    read_ref,
    step_ref,
    bias_out,
    decay_out,
    skip_out,
    state_ref,
    up_in,
    up_out,
    down_in,
    down_out,
    t_out,
    x1_in,
    u2_out,
    x2_in,
    u_out,
    y1_in,
    v2_out,
    y2_in,
    f_buf,
    entering,
    zlam,
    xlam,
    ylam,
    coef,
    column_sums,
    plane_sums,
    wide_w,
    wide_f,
    y_ref,
    dx_ref,
    dg_ref,
    stack_w,
    stack_f,
    stack_l,
    stack_m,
    row_l,
    row_m,
    gram,
    gram_t,
    mask,
    mask_t,
    b_t,
    c_t,
    db,
    dc,
    rows_r,
    rows_v,
    row_last,
    row_skip,
    gains,
    lam_ref,
    send_sem,
    recv_sem,
    small_send,
    small_recv,
):
    y, x, z = place()
    core = lax.axis_index("dp")
    barrier = pltpu.get_barrier_semaphore()
    along_z = [at(y, x, (z + k) % NZ) for k in range(1, NZ)]
    along_x = [at(y, (x + k) % NX, z) for k in range(1, NX)]
    along_y = [at((y + k) % NY, x, z) for k in range(1, NY)]
    column = core * NZ + z
    cell = y * NX + x
    in_column = []
    for k in range(1, 2 * NZ):
        other = (column + k) % (2 * NZ)
        in_column.append((other // NZ, cell * NZ + other % NZ))
    in_plane = []
    for k in range(1, NX * NY):
        other = (cell + k) % (NX * NY)
        in_plane.append((core, other * NZ + z))
    peers = in_column + in_plane
    for peer in peers:
        pl.semaphore_signal(barrier, inc=1, device_id=peer, device_id_type=MESH)

    def gather_copy(table, slot, target, k):
        return pltpu.make_async_remote_copy(
            src_ref=table.at[slot],
            dst_ref=table.at[slot],
            send_sem=small_send.at[k],
            recv_sem=small_recv.at[k],
            device_id=target,
            device_id_type=MESH,
        )

    def gather_start(table, own, value, targets, offset):
        table[own] = value
        for k, target in enumerate(targets):
            gather_copy(table, own, target, offset + k).start()

    def gather_end(table, own, size, targets, offset):
        for k, target in enumerate(targets):
            gather_copy(table, (own + size - 1 - k) % size, target, offset + k).wait_recv()

    def gather_sent(table, own, targets, offset):
        for k, target in enumerate(targets):
            gather_copy(table, own, target, offset + k).wait_send()

    one = jnp.ones((PAD, 128), F32)
    zero = jnp.zeros((PAD, 128), F32)

    def products(table, own, size):
        below, above = one, one
        for k in range(size):
            below *= jnp.where(own > k, table[k], one)
            above *= jnp.where(own < k, table[k], one)
        return below, above

    shifted, stride, rate = steps(logit_ref[...], bias_ref[...], decay_ref[...])
    upper = (iota((LEN, LEN), 0) <= iota((LEN, LEN), 1)).astype(F32)
    total = jnp.dot(stride * rate, upper, precision=EXACT, preferred_element_type=F32)
    last = total[:, LEN - 1 : LEN]

    start = lax.axis_index("ctx") * LEN
    seg_row = jnp.zeros((1, LEN), jnp.int32)
    seg_col = jnp.zeros((LEN, 128), jnp.int32)
    entry = jnp.int32(0)
    final = jnp.int32(0)
    for d in range(docs_ref.shape[1]):
        doc = docs_ref[0, d] - start
        seg_row += (doc <= iota((1, LEN), 1)).astype(jnp.int32)
        seg_col += (doc <= iota((LEN, 128), 0)).astype(jnp.int32)
        entry += (doc <= -1).astype(jnp.int32)
        final += (doc <= LEN - 1).astype(jnp.int32)
    linked = (final == entry).astype(F32)
    lam_ref[...] = pair_rows(jnp.exp(last) * linked)

    pl.semaphore_wait(barrier, len(peers))
    gather_start(zlam, z, lam_ref[...], along_z, 0)

    seg_col = seg_col[:, 0:1]
    same = seg_col == seg_row
    mask[...] = jnp.where(same & (iota((LEN, LEN), 0) >= iota((LEN, LEN), 1)), 0.0, NEG)
    mask_t[...] = jnp.where(same & (iota((LEN, LEN), 0) <= iota((LEN, LEN), 1)), 0.0, NEG)
    keep = (seg_row == entry).astype(F32)
    own = (seg_row == final).astype(F32)
    moved = total - jnp.log(stride)
    row_l[...] = total
    row_m[...] = moved
    stack_w[...] = stacked(own * jnp.exp(last - total) * stride)
    stack_f[...] = stacked(keep * jnp.exp(total))
    stack_l[...] = stacked(total)
    stack_m[...] = stacked(moved)
    b = b_ref[...]
    c = c_ref[...]
    gram[...] = mm_nt(c, b)
    gram_t[...] = mm_nt(b, c)
    b_t[...] = b.astype(F32).T.astype(BF16)
    c_t[...] = c.astype(F32).T.astype(BF16)
    dg_ref[...] = jnp.zeros((LEN, LEN), F32)
    gains[...] = pair_rows(to_column(skip_ref[...]))
    db[...] = jnp.zeros_like(db)
    dc[...] = jnp.zeros_like(dc)
    row_last[...] = jnp.zeros_like(row_last)
    row_skip[...] = jnp.zeros_like(row_skip)

    @pl.when(z == 0)
    def _():
        up_in[...] = jnp.zeros_like(up_in)

    @pl.when(z == NZ - 1)
    def _():
        down_in[...] = jnp.zeros_like(down_in)

    for d in range(2):
        coef[d, 0] = lam_ref[...]
        coef[d, 1] = one

    def gather_first():
        gather_end(zlam, z, NZ, along_z, 0)
        below_z, above_z = products(zlam, z, NZ)
        coef[0, 1] = above_z
        coef[1, 1] = below_z
        gather_start(xlam, x, below_z * above_z * lam_ref[...], along_x, 7)

    def ring_of_four(table, own):
        mine, other = table[own], table[partner(own)]
        both = mine * other
        across = table[3 - own] * table[partner(3 - own)]
        odd = own % 2 == 1
        upper = own >= 2
        forward = (
            jnp.where(odd, one, other),
            jnp.where(odd, mine, one),
            jnp.where(odd, one, zero),
            jnp.where(upper, one, across),
            jnp.where(upper, both, one),
            jnp.where(upper, jnp.where(odd, other, one), zero),
        )
        backward = (
            jnp.where(odd, other, one),
            jnp.where(odd, one, mine),
            jnp.where(odd, zero, one),
            jnp.where(upper, across, one),
            jnp.where(upper, one, both),
            jnp.where(upper, zero, jnp.where(odd, one, other)),
        )
        return forward, backward

    def put(d, k, values):
        for value in values:
            coef[d, k] = value
            k += 1

    def gather_mid():
        gather_end(xlam, x, NX, along_x, 7)
        below_x, above_x = products(xlam, x, NX)
        gather_start(ylam, y, below_x * above_x * xlam[x], along_y, 10)
        in_x = ring_of_four(xlam, x)
        for d in range(2):
            put(d, 2, (in_x[d][0], in_x[d][1], in_x[d][3], in_x[d][4]))
            put(d, 8, (in_x[d][2], in_x[d][5]))

    def gather_last():
        gather_end(ylam, y, NY, along_y, 10)
        below_x, above_x = products(xlam, x, NX)
        in_y = ring_of_four(ylam, y)
        for d in range(2):
            outer_x = below_x if d == 0 else above_x
            put(d, 6, (in_y[d][0], in_y[d][1]))
            put(d, 10, (outer_x * in_y[d][2], outer_x * in_y[d][5]))

    to_up = at(y, x, (z + 1) % NZ)
    to_down = at(y, x, (z + NZ - 1) % NZ)
    to_x1 = at(y, partner(x), z)
    to_x2 = at(y, 3 - x, z)
    to_y1 = at(partner(y), x, z)
    to_y2 = at(3 - y, x, z)

    def link(stage, c, source, target, device):
        return pltpu.make_async_remote_copy(
            src_ref=source.at[c],
            dst_ref=target.at[c],
            send_sem=send_sem.at[stage, c],
            recv_sem=recv_sem.at[stage, c],
            device_id=device,
            device_id_type=MESH,
        )

    links = (
        functools.partial(link, 0, source=up_out, target=up_in, device=to_up),
        functools.partial(link, 1, source=down_out, target=down_in, device=to_down),
        functools.partial(link, 2, source=t_out, target=x1_in, device=to_x1),
        functools.partial(link, 3, source=u2_out, target=x2_in, device=to_x2),
        functools.partial(link, 4, source=u_out, target=y1_in, device=to_y1),
        functools.partial(link, 5, source=v2_out, target=y2_in, device=to_y2),
    )

    def staged(n):
        return (n >= 0) & (n < SET)

    def chunk(n, second):
        return 4 * (n // 2) + n % 2 + 2 * second

    def outside(c, d):
        return (row(d, 8, c) * x1_in[c, d] + row(d, 9, c) * x2_in[c, d]) + (
            row(d, 10, c) * y1_in[c, d] + row(d, 11, c) * y2_in[c, d]
        )

    lag_t = HOP * jnp.maximum(z, NZ - 1 - z)
    first = iota((LEN, 128), 1) < HALF

    def row(d, k, c):
        return coef[d, k, pl.ds(c // SPLIT, 1), :]

    def begin_pair(j):
        lanes = pl.ds(pl.multiple_of(j * 128, 128), 128)
        expand = spread(j)
        w = mm(stack_w[...], expand)
        f = mm(stack_f[...], expand)
        wide_w[:, lanes] = w
        wide_f[:, lanes] = f
        high, low = split2(w * x_ref[:, lanes].astype(F32))
        state = mm(b_t[...], high) + mm(b_t[...], low)
        high, low = split2(f * dy_ref[:, lanes].astype(F32))
        state_b = mm(c_t[...], high) + mm(c_t[...], low)
        for k in range(SPLIT):
            state_ref[SPLIT * j + k, 0] = state[k * ROWS : (k + 1) * ROWS]
            state_ref[SPLIT * j + k, 1] = state_b[k * ROWS : (k + 1) * ROWS]

    def mix_head(h):
        j = h // 2
        second = h % 2 == 1
        lanes = pl.ds(pl.multiple_of(j * 128, 128), 128)
        xs = x_ref[:, lanes]
        dys = dy_ref[:, lanes]
        expand = spread(j)
        columns_l = mm(stack_l[...], expand)
        columns_m = mm(stack_m[...], expand)
        lrow = row_l[pl.ds(h, 1), :]
        mrow = row_m[pl.ds(h, 1), :]
        lcol = jnp.where(second, columns_l[:, HALF : HALF + 1], columns_l[:, 0:1])
        mcol = jnp.where(second, columns_m[:, HALF : HALF + 1], columns_m[:, 0:1])
        ours = first != second
        decays = jnp.exp((lcol - mrow) + mask[...])
        high, low = split2(decays * gram[...])
        y_ref[:, lanes] = jnp.where(ours, mm(high, xs) + mm(low, xs), y_ref[:, lanes])
        part = jnp.where(ours, dys, jnp.zeros_like(dys))
        dg_ref[...] += mm_nt(part, xs) * decays
        decays_t = jnp.exp((lrow - mcol) + mask_t[...])
        high, low = split2(decays_t * gram_t[...])
        dx_ref[:, lanes] = jnp.where(ours, mm(high, dys) + mm(low, dys), dx_ref[:, lanes])

    def finish_pair(j):
        lanes = pl.ds(pl.multiple_of(j * 128, 128), 128)
        state_in, adjoint = entering[0], entering[1]
        state_end = jnp.concatenate([state_ref[SPLIT * j + k, 0] for k in range(SPLIT)], axis=0)
        xs = x_ref[:, lanes].astype(F32)
        dys = dy_ref[:, lanes].astype(F32)
        w = wide_w[:, lanes]
        f = wide_f[:, lanes]
        gain = gains[pl.ds(j, 1), :]
        s_high, s_low = split2(state_in)
        a_high, a_low = split2(adjoint)
        inner = y_ref[:, lanes] + f * (mm(c_ref[...], s_high) + mm(c_ref[...], s_low))
        inner_t = dx_ref[:, lanes] + w * (mm(b_ref[...], a_high) + mm(b_ref[...], a_low))
        mixed_ref[:, lanes] = (inner + gain * xs).astype(BF16)
        feature_ref[:, lanes] = (inner_t + gain * dys).astype(BF16)
        select = (iota((8, 128), 1) // HALF == iota((8, 128), 0)).astype(BF16)
        high, middle, low = split3(dys * inner)
        r = mm_nt(select, high) + (mm_nt(select, middle) + mm_nt(select, low))
        high, middle, low = split3(xs * inner_t)
        v = mm_nt(select, high) + (mm_nt(select, middle) + mm_nt(select, low))
        for k in range(2):
            rows_r[pl.ds(2 * j + k, 1), :] = r[k : k + 1]
            rows_v[pl.ds(2 * j + k, 1), :] = v[k : k + 1]
        high, low = split2(f * dys)
        dc[...] += mm_nt(high, s_high) + (mm_nt(high, s_low) + mm_nt(low, s_high))
        high, low = split2(w * xs)
        db[...] += mm_nt(high, a_high) + (mm_nt(high, a_low) + mm_nt(low, a_high))
        row_skip[pl.ds(j, 1), :] = jnp.sum(dys * xs, axis=0, keepdims=True)
        leaving = lam_ref[pl.ds(j, 1), :] * state_in + state_end
        row_last[pl.ds(j, 1), :] = jnp.sum(adjoint * leaving, axis=0, keepdims=True)

    def tick(i, carry):
        @pl.when(i == GATHER_Z)
        def _():
            gather_first()

        @pl.when(i == GATHER_X)
        def _():
            gather_mid()

        @pl.when(i == GATHER_Y)
        def _():
            gather_last()

        @pl.when(i < PAIRS)
        def _():
            begin_pair(i)

        def chains(second):
            since = i - (LATER + 4 * HOP) * second
            n = since - HOP * z

            @pl.when(staged(n))
            def _(second=second, n=n):
                c = chunk(n, second)

                @pl.when(z > 0)
                def _():
                    links[0](c).wait_recv()

                if second:
                    ahead = up_in[c, 0] + row(1, 1, c) * f_buf[c, 0]
                    up_out[c, 0] = row(0, 0, c) * ahead + state_ref[c, 0]
                    up_out[c, 1] = up_in[c, 1] + f_buf[c, 1]
                else:
                    up_out[c, 0] = row(0, 0, c) * up_in[c, 0] + state_ref[c, 0]
                    up_out[c, 1] = up_in[c, 1] + row(1, 1, c) * state_ref[c, 1]

                @pl.when(z < NZ - 1)
                def _():
                    links[0](c).start()

            n = since - HOP * (NZ - 1 - z)

            @pl.when(staged(n))
            def _(second=second, n=n):
                c = chunk(n, second)

                @pl.when(z < NZ - 1)
                def _():
                    links[1](c).wait_recv()

                if second:
                    ahead = down_in[c, 1] + row(0, 1, c) * f_buf[c, 1]
                    down_out[c, 0] = down_in[c, 0] + f_buf[c, 0]
                    down_out[c, 1] = row(1, 0, c) * ahead + state_ref[c, 1]
                else:
                    down_out[c, 0] = down_in[c, 0] + row(0, 1, c) * state_ref[c, 0]
                    down_out[c, 1] = row(1, 0, c) * down_in[c, 1] + state_ref[c, 1]

                @pl.when(z > 0)
                def _():
                    links[1](c).start()

        def exchanges(second):
            first_at = i - LATER if second else i - lag_t

            @pl.when(staged(first_at))
            def _(second=second, first_at=first_at):
                c = chunk(first_at, second)
                if second:
                    t_out[c, 0] = row(0, 1, c) * state_ref[c, 0]
                    t_out[c, 1] = row(1, 1, c) * state_ref[c, 1]
                else:
                    t_out[c, 0] = up_out[c, 0] * row(0, 1, c) + down_in[c, 0]
                    t_out[c, 1] = down_out[c, 1] * row(1, 1, c) + up_in[c, 1]
                links[2](c).start()

            for stage, mine, came, result, k in (
                (2, t_out, x1_in, u2_out, 2),
                (3, u2_out, x2_in, u_out, 4),
                (4, u_out, y1_in, v2_out, 6),
            ):
                n = first_at - HOP * (stage - 1)

                @pl.when(staged(n))
                def _(stage=stage, mine=mine, came=came, result=result, k=k, n=n, second=second):
                    c = chunk(n, second)
                    links[stage](c).wait_recv()
                    for d in range(2):
                        result[c, d] = row(d, k, c) * mine[c, d] + row(d, k + 1, c) * came[c, d]
                    links[stage + 1](c).start()

            n = first_at - HOP * 4

            @pl.when(staged(n))
            def _(second=second, n=n):
                c = chunk(n, second)
                links[5](c).wait_recv()
                for d in range(2):
                    f_buf[c, d] = outside(c, d)

        chains(0)
        exchanges(1)
        chains(1)
        exchanges(0)

        @pl.when(i < HEADS)
        def _():
            mix_head(i)

        for second in (0, 1):
            n = i - lag_t - HOP * 4 - LATER * second

            @pl.when(staged(n) & (n % 2 == 1))
            def _(second=second, n=n):
                for k in range(2):
                    c = chunk(n - 1 + k, second)
                    lines = slice(k * ROWS, (k + 1) * ROWS)
                    if second:
                        entering[0, lines] = up_in[c, 0] + row(1, 1, c) * (down_in[c, 0] + f_buf[c, 0])
                        entering[1, lines] = down_in[c, 1] + row(0, 1, c) * (up_in[c, 1] + f_buf[c, 1])
                    else:
                        entering[0, lines] = up_in[c, 0] + row(1, 1, c) * f_buf[c, 0]
                        entering[1, lines] = down_in[c, 1] + row(0, 1, c) * f_buf[c, 1]

        done_at = i - lag_t - HOP * 4
        second = 1 - done_at % 2
        n = done_at - LATER * second

        @pl.when(staged(n))
        def _():
            finish_pair(2 * (n // 2) + second)

        return carry

    lax.fori_loop(0, SET + HOP * (NZ - 1 + 4) + LATER, tick, 0)

    dg = dg_ref[...]
    high, low = split2(dg)
    read_ref[...] = (dc[...] + (mm(high, b_ref[...]) + mm(low, b_ref[...]))).astype(BF16)
    high, low = split2(dg.T)
    write_ref[...] = (db[...] + (mm(high, c_ref[...]) + mm(low, c_ref[...]))).astype(BF16)

    shifted, stride, rate = steps(logit_ref[...], bias_ref[...], decay_ref[...])
    v = rows_v[...]
    is_last = iota((HEADS, LEN), 1) == LEN - 1
    slope = rows_r[...] - v + jnp.where(is_last, unpair_sums(row_last[...]), 0.0)
    lower = (iota((LEN, LEN), 0) >= iota((LEN, LEN), 1)).astype(F32)
    slope = jnp.dot(slope, lower, precision=EXACT, preferred_element_type=F32)
    step = (v / stride + rate * slope) * (1.0 / (1.0 + jnp.exp(-shifted)))
    step_ref[...] = step
    bias_sum = jnp.sum(step, axis=1, keepdims=True)
    decay_sum = jnp.sum(slope * (rate * stride), axis=1, keepdims=True)
    skip_sum = unpair_sums(row_skip[...])
    sums = jnp.concatenate(
        [to_row(bias_sum), to_row(decay_sum), to_row(skip_sum), jnp.zeros((5, 128), F32)], axis=0
    )
    gather_start(column_sums, column, sums, in_column, 13)

    def drain(c, carry):
        @pl.when(z < NZ - 1)
        def _():
            links[0](c).wait_send()

        @pl.when(z > 0)
        def _():
            links[1](c).wait_send()

        for stage in range(2, 6):
            links[stage](c).wait_send()
        return carry

    lax.fori_loop(0, CHUNKS, drain, 0)
    gather_end(column_sums, column, 2 * NZ, in_column, 13)
    gather_start(plane_sums, cell, jnp.sum(column_sums[...], axis=0), in_plane, 28)
    gather_end(plane_sums, cell, NX * NY, in_plane, 28)
    sums = jnp.sum(plane_sums[...], axis=0)
    bias_out[...] = sums[0:1, :HEADS]
    decay_out[...] = sums[1:2, :HEADS]
    skip_out[...] = sums[2:3, :HEADS]

    gather_sent(zlam, z, along_z, 0)
    gather_sent(xlam, x, along_x, 7)
    gather_sent(ylam, y, along_y, 10)
    gather_sent(column_sums, column, in_column, 13)
    gather_sent(plane_sums, cell, in_plane, 28)


def emit_kernel(*refs):
    count = len(refs) // 2
    for k in range(count):
        refs[count + k][...] = refs[k][...]


VM = pl.BlockSpec(memory_space=pltpu.VMEM)
SM = pl.BlockSpec(memory_space=pltpu.SMEM)


def shape(dims, kind=F32):
    return jax.ShapeDtypeStruct(dims, kind)


def local(
    features,
    write_keys,
    read_queries,
    step_logits,
    step_bias,
    decay_log,
    skip_gain,
    doc_starts,
    out_grad,
):
    x, b, c, logits, dy = features[0], write_keys[0], read_queries[0], step_logits[0], out_grad[0]
    bias, decay, skip = step_bias[None], decay_log[None], skip_gain[None]
    carry_shape = (CHUNKS, 2, ROWS, 128)
    outputs = pl.pallas_call(
        layer_kernel,
        out_shape=(
            shape((LEN, WIDE), BF16),
            shape((LEN, WIDE), BF16),
            shape((LEN, 128), BF16),
            shape((LEN, 128), BF16),
            shape((HEADS, LEN)),
            shape((1, HEADS)),
            shape((1, HEADS)),
            shape((1, HEADS)),
        ),
        in_specs=[SM] + [VM] * 8,
        out_specs=(VM,) * 8,
        scratch_shapes=[pltpu.VMEM(carry_shape, F32)] * 14
        + [pltpu.VMEM((2, 128, 128), F32)]
        + [pltpu.VMEM((n, PAD, 128), F32) for n in (NZ, NX, NY)]
        + [pltpu.VMEM((2, 12, PAD, 128), F32)]
        + [pltpu.VMEM((n, 8, 128), F32) for n in (2 * NZ, NX * NY)]
        + [pltpu.VMEM((LEN, WIDE), F32)] * 4
        + [pltpu.VMEM((LEN, LEN), F32)]
        + [pltpu.VMEM((LEN, 128), BF16)] * 4
        + [pltpu.VMEM((HEADS, LEN), F32)] * 2
        + [pltpu.VMEM((LEN, LEN), F32)] * 4
        + [pltpu.VMEM((128, LEN), BF16)] * 2
        + [pltpu.VMEM((LEN, 128), F32)] * 2
        + [pltpu.VMEM((HEADS, LEN), F32)] * 2
        + [pltpu.VMEM((PAD, 128), F32)] * 4
        + [pltpu.SemaphoreType.DMA((6, CHUNKS))] * 2
        + [pltpu.SemaphoreType.DMA((43,))] * 2,
        compiler_params=pltpu.CompilerParams(
            collective_id=0, has_side_effects=True, vmem_limit_bytes=60 * 2**20
        ),
        name="layer",
    )(doc_starts, x, dy, b, c, logits, bias, decay, skip)
    outputs = pl.pallas_call(
        emit_kernel,
        out_shape=tuple(shape(o.shape, o.dtype) for o in outputs),
        in_specs=[VM] * 8,
        out_specs=(VM,) * 8,
        name="emit",
    )(*outputs)
    mixed, feature_grad, write_grad, read_grad, step_grad, bias_sum, decay_sum, skip_sum = outputs
    return (
        mixed[None],
        feature_grad[None],
        write_grad[None],
        read_grad[None],
        step_grad[None],
        bias_sum[0],
        decay_sum[0],
        skip_sum[0],
    )


def solution(mesh):
    in_specs = (
        P("dp", "ctx", None),
        P("dp", "ctx", None),
        P("dp", "ctx", None),
        P("dp", None, "ctx"),
        P(),
        P(),
        P(),
        P("dp", None),
        P("dp", "ctx", None),
    )
    out_specs = (
        P("dp", "ctx", None),
        P("dp", "ctx", None),
        P("dp", "ctx", None),
        P("dp", "ctx", None),
        P("dp", None, "ctx"),
        P(),
        P(),
        P(),
    )
    return jax.shard_map(local, mesh=mesh, in_specs=in_specs, out_specs=out_specs, check_vma=False)
```
